128 devices in a mesh: tile: 128 (over z, x, y, core).
Axes of the slice: x: 4, y: 4, z: 4, core: 2. Of those that a mesh axis runs over, the one named last changes fastest.
Arguments:
- air_state: float32 [8, 1024, 128], P(None, 'tile'), may hold values from -6 to 6
- sea_state: float32 [48, 256, 512], P(None, 'tile'), may hold values from -6 to 6
- flux_start: float32 [4, 1024, 128], P(None, 'tile'), may hold values from -6 to 6
- air_cells: int32 [128, 5, 1024], P('tile'), may hold values from 0 to 1023
- sea_cells: int32 [128, 5, 1024], P('tile'), may hold values from 0 to 1023
- slot_counts: int32 [128, 5], P('tile'), may hold values from 0 to 1024, as said below
- sea_share: float32 [128, 5, 1024], P('tile'), may hold values from 0.2 to 1
- air_share: float32 [128, 5, 1024], P('tile'), may hold values from 0.2 to 1
- polar_fold_partner: int32 [512], replicated, may hold values from 0 to 511, each once
- wet_mask: int32 [256, 512], P('tile'), may hold values 0 or 1
- air_cotangent: float32 [8, 1024, 128], P(None, 'tile'), may hold values from -6 to 6
- sea_cotangent: float32 [48, 256, 512], P(None, 'tile'), may hold values from -6 to 6
- air_encoder: bfloat16 [64, 81], replicated, may hold values from -0.625 to 0.625
- air_depthwise: bfloat16 [64, 9], replicated, may hold values from -2 to 2
- air_expand: bfloat16 [256, 64], replicated, may hold values from -0.75 to 0.75
- air_contract: bfloat16 [64, 256], replicated, may hold values from -0.375 to 0.375
- air_decoder: bfloat16 [12, 64], replicated, may hold values from -0.75 to 0.75
- sea_encoder: bfloat16 [64, 468], replicated, may hold values from -0.25 to 0.25
- sea_depthwise: bfloat16 [64, 9], replicated, may hold values from -2 to 2
- sea_expand: bfloat16 [256, 64], replicated, may hold values from -0.75 to 0.75
- sea_contract: bfloat16 [64, 256], replicated, may hold values from -0.375 to 0.375
- sea_decoder: bfloat16 [48, 64], replicated, may hold values from -0.75 to 0.75
Outputs:
- air_final: float32 [8, 1024, 128], P(None, 'tile')
- sea_final: float32 [48, 256, 512], P(None, 'tile')
- air_grad: float32 [8, 1024, 128], P(None, 'tile')
- sea_grad: float32 [48, 256, 512], P(None, 'tile')
- flux_grad: float32 [4, 1024, 128], P(None, 'tile')
- air_encoder_grad: float32 [64, 81], replicated
- air_depthwise_grad: float32 [64, 9], replicated
- air_expand_grad: float32 [256, 64], replicated
- air_contract_grad: float32 [64, 256], replicated
- air_decoder_grad: float32 [12, 64], replicated
- sea_encoder_grad: float32 [64, 468], replicated
- sea_depthwise_grad: float32 [64, 9], replicated
- sea_expand_grad: float32 [256, 64], replicated
- sea_contract_grad: float32 [64, 256], replicated
- sea_decoder_grad: float32 [48, 64], replicated
The draws below stay inside these ranges and needn't reach their ends.
Inputs may be any that keep to these rules, and one draw needn't show every extreme that they name: `slot_counts`: the number of used slots of each block, from its first slot on; 0 exactly for blocks whose atmosphere band lies off the grid, at least 256 for all others; in every draw some ocean band has 1024 used slots in every block with an atmosphere band on the grid, and some atmosphere band has 1024 used slots with every ocean band that it is paired with. `air_cells`: a cell of atmosphere band a, numbered row * 128 + column within the band. `sea_cells`: a cell of ocean band o, numbered row * 512 + column within the band. `polar_fold_partner`: each column appears once. `wet_mask`: 1 at ocean cells, 0 on land.
All inputs are finite; a program needn't handle non-finite values. No bound on the sum of `wet_mask` on one device may be relied on, other than what follows from the above.
Results may differ from the reference program's by a relative error of at most 0.025.
Values may be sent and summed in bfloat16 or wider, within the bound.
A program may use at most 128 MiB of HBM per device.

```python
import math
import jax
import jax.numpy as jnp
from jax import lax

C = 64
HID = 256
ACH = 8
NF = 4
STEPS = 2
NEAR = 5
AIR_LONGITUDES = 128
OCOL = 512
SLOTS = 1024
OCH = 48
AIRSTRIP_SITES = 1024
OCELLS = 1024
AIR_LATITUDES = 1024
ONROWS = 256
N_TILE = 128


def draw_slot_counts(key, part):
    first_key, second_key, third_key = jax.random.split(jax.random.fold_in(key, 17), 3)
    lowest = max(1, SLOTS // 4)
    counts = jax.random.randint(first_key, (N_TILE, NEAR), lowest, SLOTS + 1)
    full_ocean = jax.random.randint(second_key, (), 0, N_TILE)
    full_air = jax.random.randint(third_key, (), 0, N_TILE)
    bands = jnp.arange(N_TILE)
    partner_band = bands[:, None] + jnp.arange(NEAR)[None, :] - (NEAR - 1) // 2
    counts = jnp.where(bands[:, None] == full_ocean, SLOTS, counts)
    counts = jnp.where(partner_band == full_air, SLOTS, counts)
    inside = (partner_band >= 0) & (partner_band < N_TILE)
    counts = jnp.where(inside, counts, 0)
    return counts.astype(jnp.int32)


def place_ends(result, key, least, largest):
    index_at = [jax.random.randint(jax.random.fold_in(key, axis), (), 0, length) for axis, length in enumerate(result.shape)]
    longest = result.shape.index(max(result.shape))
    beside = index_at[:longest] + [(index_at[longest] + 1) % result.shape[longest]] + index_at[longest + 1:]
    return result.at[tuple(index_at)].set(least).at[tuple(beside)].set(largest)


def block_scale(rng, extent, cuts, smallest, top_value):
    factor_of = 1.0
    for position, parts in cuts:
        steps = jax.random.uniform(jax.random.fold_in(jax.random.fold_in(rng, 6), position), (parts,), jnp.float32, smallest / len(cuts), top_value / len(cuts))
        factor_of = factor_of * jnp.repeat(jnp.exp(steps), extent[position] // parts).reshape((-1,) + (1,) * (len(extent) - 1 - position))
    return factor_of


def bell_draw(stream_key, dims, deviation, most, cuts=(), held_as=jnp.bfloat16):
    drawn = deviation * jax.random.normal(stream_key, dims, jnp.float32)
    if cuts:
        drawn = drawn * block_scale(stream_key, dims, cuts, -0.22, 0.18)
    return jnp.clip(drawn, -most, most).astype(held_as)


def setup_inputs(seed: int = 0) -> dict:
    key_of = jax.random.split(jax.random.key(seed), 23)
    return {
        "air_state": bell_draw(key_of[0], (ACH, AIR_LATITUDES, AIR_LONGITUDES), 1.0, 6.0, ((1, 128),), jnp.float32),
        "sea_state": bell_draw(key_of[1], (OCH, ONROWS, OCOL), 1.0, 6.0, ((1, 128),), jnp.float32),
        "flux_start": bell_draw(key_of[2], (NF, AIR_LATITUDES, AIR_LONGITUDES), 1.0, 6.0, ((1, 128),), jnp.float32),
        "air_cells": place_ends(jax.random.randint(key_of[3], (N_TILE, NEAR, SLOTS), 0, AIRSTRIP_SITES), jax.random.fold_in(key_of[3], 1), 0, AIRSTRIP_SITES - 1).astype(jnp.int32),
        "sea_cells": place_ends(jax.random.randint(key_of[4], (N_TILE, NEAR, SLOTS), 0, OCELLS), jax.random.fold_in(key_of[4], 1), 0, OCELLS - 1).astype(jnp.int32),
        "slot_counts": draw_slot_counts(jax.random.fold_in(key_of[22], 71), 0),
        "sea_share": jnp.clip(0.2 + 0.8 * jax.random.uniform(key_of[6], (N_TILE, NEAR, SLOTS), jnp.float32) ** block_scale(key_of[6], (N_TILE, NEAR, SLOTS), ((0, 128),), -0.2, 0.2), 0.2, 1.0),
        "air_share": jnp.clip(0.2 + 0.8 * jax.random.uniform(key_of[7], (N_TILE, NEAR, SLOTS), jnp.float32) ** block_scale(key_of[7], (N_TILE, NEAR, SLOTS), ((0, 128),), -0.2, 0.2), 0.2, 1.0),
        "polar_fold_partner": jax.random.permutation(key_of[8], OCOL).astype(jnp.int32),
        "wet_mask": place_ends((jax.random.randint(key_of[9], (ONROWS, OCOL), 0, 3) < 2).astype(jnp.int32), jax.random.fold_in(key_of[9], 1), 0, 1),
        "air_cotangent": bell_draw(key_of[10], (ACH, AIR_LATITUDES, AIR_LONGITUDES), 1.0, 6.0, ((1, 128),), jnp.float32),
        "sea_cotangent": bell_draw(key_of[11], (OCH, ONROWS, OCOL), 1.0, 6.0, ((1, 128),), jnp.float32),
        "air_encoder": bell_draw(key_of[12], (C, 9 * (ACH + 1)), (9 * (ACH + 1)) ** -0.5, 0.625),
        "air_depthwise": bell_draw(key_of[13], (C, 9), 9 ** -0.5, 2.0),
        "air_expand": bell_draw(key_of[14], (HID, C), C ** -0.5, 0.75),
        "air_contract": bell_draw(key_of[15], (C, HID), HID ** -0.5, 0.375),
        "air_decoder": bell_draw(key_of[16], (ACH + NF, C), C ** -0.5, 0.75),
        "sea_encoder": bell_draw(key_of[17], (C, 9 * (OCH + NF)), (9 * (OCH + NF)) ** -0.5, 0.25),
        "sea_depthwise": bell_draw(key_of[18], (C, 9), 9 ** -0.5, 2.0),
        "sea_expand": bell_draw(key_of[19], (HID, C), C ** -0.5, 0.75),
        "sea_contract": bell_draw(key_of[20], (C, HID), HID ** -0.5, 0.375),
        "sea_decoder": bell_draw(key_of[21], (OCH, C), C ** -0.5, 0.75),
    }


def taps(extended):
    rows = extended.shape[1] - 2
    pieces = []
    for shift_row in range(3):
        part = extended[:, shift_row:shift_row + rows]
        for shift_col in (-1, 0, 1):
            pieces.append(jnp.roll(part, -shift_col, axis=2))
    return pieces

def encode(encoder, extended):
    stacked = jnp.concatenate(taps(extended), axis=0)
    inputs, rows, width = stacked.shape
    product = jnp.dot(encoder.astype(jnp.bfloat16), stacked.reshape(inputs, rows * width), preferred_element_type=jnp.float32)
    return product.astype(jnp.bfloat16).reshape(-1, rows, width)

def block(params, padded):
    depthwise, expand, contract, decoder = params
    pieces = taps(padded)
    mixed = pieces[0] * depthwise[:, 0][:, None, None]
    for tap in range(1, 9):
        mixed = mixed + pieces[tap] * depthwise[:, tap][:, None, None]
    channels, rows, width = mixed.shape
    flat = mixed.reshape(channels, rows * width)
    centred = flat - lax.optimization_barrier(jnp.mean(flat, axis=0, keepdims=True))
    normed = centred * lax.rsqrt(lax.optimization_barrier(jnp.mean(centred * centred, axis=0, keepdims=True)) + 1e-06)
    hidden = jax.nn.gelu(jnp.dot(expand.astype(jnp.bfloat16), normed.astype(jnp.bfloat16), preferred_element_type=jnp.float32), approximate=True).astype(jnp.bfloat16)
    residual = padded[:, 1:-1].reshape(channels, rows * width) + jnp.dot(contract.astype(jnp.bfloat16), hidden, preferred_element_type=jnp.float32)
    output = jnp.dot(decoder.astype(jnp.bfloat16), residual.astype(jnp.bfloat16), preferred_element_type=jnp.float32)
    return output.reshape(-1, rows, width)

def band_model(weights, extended, first, last, folded, partner):
    features = encode(weights[0], extended).astype(jnp.float32)
    features = features.at[:, 0].set(jnp.where(first, 0.0, features[:, 0]))
    if folded:
        top = features[:, -2][:, partner]
    else:
        top = jnp.zeros_like(features[:, -1])
    features = features.at[:, -1].set(jnp.where(last, top, features[:, -1]))
    return block(weights[1:], features)

def run_joined_climate(weights, field, folded, partner):
    lowered = field.astype(jnp.bfloat16)
    inputs, total, width = lowered.shape
    if folded:
        top = jnp.stack([lowered[:, total - 1][:, partner], lowered[:, total - 2][:, partner]], axis=1)
    else:
        top = jnp.zeros((inputs, 2, width), lowered.dtype)
    padded = jnp.concatenate([jnp.zeros((inputs, 2, width), lowered.dtype), lowered, top], axis=1)
    rows = total // N_TILE

    def one_band(band):
        extended = lax.dynamic_slice_in_dim(padded, band * rows, rows + 4, 1)
        return band_model(weights, extended, band == 0, band == N_TILE - 1, folded, partner)
    bands = lax.map(jax.checkpoint(one_band), jnp.arange(N_TILE, dtype=jnp.int32))
    return jnp.transpose(bands, (1, 0, 2, 3)).reshape(bands.shape[1], total, width)

def reference(air_state, sea_state, flux_start, air_cells, sea_cells, slot_counts, sea_share, air_share, polar_fold_partner, wet_mask, air_cotangent, sea_cotangent, air_encoder, air_depthwise, air_expand, air_contract, air_decoder, sea_encoder, sea_depthwise, sea_expand, sea_contract, sea_decoder):
    bands = jnp.arange(N_TILE, dtype=jnp.int32)
    blocks = jnp.arange(NEAR, dtype=jnp.int32)
    partner_band = jnp.clip(bands[:, None] + blocks[None, :] - (NEAR - 1) // 2, 0, N_TILE - 1).astype(jnp.int32)
    air_for_block = air_cells[partner_band, blocks[None, :], :]
    air_global_mesh = (partner_band[:, :, None] * AIRSTRIP_SITES + air_for_block).reshape(-1)
    marine_global_mesh = (bands[:, None, None] * OCELLS + sea_cells).reshape(-1)
    used = (jnp.arange(SLOTS, dtype=jnp.int32)[None, None, :] < slot_counts[:, :, None]).astype(jnp.float32)
    interpolate_to_sky = (air_share * used).reshape(-1)
    toward_sea = (sea_share * used).reshape(-1)
    wet = wet_mask.astype(jnp.float32)

    def rollout(air_present_state, sea_now, flux_now, air_learned_tensors, sea_params):
        for step in range(STEPS):
            interface_transfer_map = sea_now[0].reshape(-1)
            skin_heat_level = jnp.zeros((N_TILE * AIRSTRIP_SITES,), jnp.float32).at[air_global_mesh].add(interpolate_to_sky * interface_transfer_map[marine_global_mesh])
            flux_flat = flux_now.reshape(NF, -1)
            inbound_energy_map = jnp.zeros((NF, N_TILE * OCELLS), jnp.float32).at[:, marine_global_mesh].add(toward_sea[None] * flux_flat[:, air_global_mesh])
            air_result_state = run_joined_climate(air_learned_tensors, jnp.concatenate([air_present_state, skin_heat_level.reshape(1, AIR_LATITUDES, AIR_LONGITUDES)], axis=0), False, polar_fold_partner)
            sea_out = run_joined_climate(sea_params, jnp.concatenate([sea_now, inbound_energy_map.reshape(NF, ONROWS, OCOL)], axis=0), True, polar_fold_partner)
            flux_now = air_result_state[ACH:]
            air_present_state = air_present_state + air_result_state[:ACH]
            sea_now = sea_now + wet[None] * sea_out
        return (air_present_state, sea_now)
    air_learned_tensors = tuple((weight.astype(jnp.float32) for weight in (air_encoder, air_depthwise, air_expand, air_contract, air_decoder)))
    sea_params = tuple((weight.astype(jnp.float32) for weight in (sea_encoder, sea_depthwise, sea_expand, sea_contract, sea_decoder)))
    finals, pullback = jax.vjp(rollout, air_state, sea_state, flux_start, air_learned_tensors, sea_params)
    air_grad, sea_grad, flux_grad, air_grads, sea_grads = pullback((air_cotangent, sea_cotangent))
    air_scale = 1.0 / math.sqrt(AIR_LATITUDES * AIR_LONGITUDES)
    sea_scale = 1.0 / math.sqrt(ONROWS * OCOL)
    return (finals[0], finals[1], air_grad, sea_grad, flux_grad, air_grads[0] * air_scale, air_grads[1] * air_scale, air_grads[2] * air_scale, air_grads[3] * air_scale, air_grads[4] * air_scale, sea_grads[0] * sea_scale, sea_grads[1] * sea_scale, sea_grads[2] * sea_scale, sea_grads[3] * sea_scale, sea_grads[4] * sea_scale)
```

```python
import math

import jax
import jax.numpy as jnp
from jax import lax
from jax.experimental import pallas as pl
from jax.experimental.pallas import tpu as pltpu
from jax.sharding import PartitionSpec as P

MESH = pl.DeviceIdType.MESH
F32 = jnp.float32
BF = jnp.bfloat16
OFFS = (-2, -1, 1, 2)
NEAR = 5
SL = 1024
C0 = math.sqrt(2.0 / math.pi)
C1 = 0.044715


def nn(a, b):
    return jnp.dot(a, b, preferred_element_type=F32)


def nt(a, b):
    return lax.dot_general(a, b, (((1,), (1,)), ((), ())), preferred_element_type=F32)


def tn(a, b):
    return lax.dot_general(a, b, (((0,), (0,)), ((), ())), preferred_element_type=F32)


def roll(x, by):
    return pltpu.roll(x, by % x.shape[1], axis=1)


class Names:
    def __init__(self, names, refs):
        for name, ref in zip(names, refs):
            setattr(self, name, ref)


class Model:
    def __init__(self, name, rows, width, state, inputs, chans, given, outs):
        self.name, self.rows, self.width = name, rows, width
        self.state, self.chans, self.outs = state, chans, outs
        self.inputs, self.given = inputs, given
        self.ext = (rows + 4) * width
        self.pad = (rows + 2) * width

    def scratch(self):
        f, b = F32, BF
        n, kc = self.name, self.chans
        return [
            (n + "_x", (kc, self.ext), f),
            (n + "_s3", (2, 3 * kc, self.ext), b),
            (n + "_y", (192, self.ext), f),
            (n + "_fp", (2, 64, self.pad), f),
            (n + "_mix", (64, SL), f),
            (n + "_nrm", (2, 64, SL), f),
            (n + "_rstd", (2, 1, SL), f),
            (n + "_dgelu", (2, 256, SL), f),
            (n + "_hid", (2, 256, SL), b),
            (n + "_resb", (2, 64, SL), b),
            (n + "_out", (self.outs, SL), f),
            (n + "_cot", (self.outs, SL), f),
            (n + "_dyb", (self.outs, SL), b),
            (n + "_dresb", (64, SL), b),
            (n + "_dpreb", (256, SL), b),
            (n + "_dmr", (3, 64, SL), f),
            (n + "_dfs", (192, self.ext), b),
            (n + "_ds3", (3 * kc, self.ext), f),
            (n + "_dx", (kc, self.ext), f),
            (n + "_encf", (192, 3 * kc), f),
            (n + "_enc", (192, 3 * kc), b),
            (n + "_enct", (3 * kc, 192), b),
            (n + "_exp", (256, 64), b),
            (n + "_cont", (256, 64), b),
            (n + "_decf", (self.outs, 64), f),
            (n + "_dec", (self.outs, 64), b),
            (n + "_dect", (64, self.outs), b),
            (n + "_dw", (64, 16), f),
        ]


AIR = Model("air", 8, 128, 8, 9, 16, 12, 16)
SEA = Model("sea", 2, 512, 48, 52, 64, 48, 48)

INPUTS = (
    "air_state",
    "sea_state",
    "flux",
    "air_cells",
    "sea_cells",
    "counts",
    "sea_share",
    "air_share",
    "partner",
    "wet",
    "air_c",
    "sea_c",
    "air_renc",
    "air_rdw",
    "air_expt",
    "air_con",
    "air_rdec",
    "sea_renc",
    "sea_rdw",
    "sea_expt",
    "sea_con",
    "sea_rdec",
)
OUTPUTS = ("o_air", "o_sea", "o_dair", "o_dsea", "o_dflux", "o_grads")
WEIGHTS = ("enc", "dw", "exp", "con", "dec")

COPIES = 80
GROWS = 1024
G_EXP, G_CON, G_ENC0, G_ENC1, G_DEC, G_DW = 0, 256, 512, 704, 896, 960


def scratch_list():
    f, b = F32, BF
    items = AIR.scratch() + SEA.scratch()
    items += [
        ("meta_pay", (4, 8, SL), f),
        ("meta_in", (NEAR, 8, SL), f),
        ("oh_aa", (128, NEAR * SL), b),
        ("oh_as", (128, NEAR * SL), b),
        ("oh_sa", (128, NEAR * SL), b),
        ("oh_ss", (128, NEAR * SL), b),
        ("fold", (512, 512), b),
        ("wetf", (1, SL), f),
        ("a_now", (8, SL), f),
        ("o_now", (48, SL), f),
        ("pay_f", (2, 32, 128), f),
        ("in_f", (2, 4, 32, 128), f),
        ("pay_s", (2, 8, 128), f),
        ("in_s", (2, 4, 8, 128), f),
        ("halo_s", (2, 48, SL), b),
        ("halo_s_in", (2, 2, 48, SL), b),
        ("halo_a", (2, 2, 8, 256), f),
        ("halo_a_in", (2, 2, 8, 256), f),
        ("pay_g", (2, 32, 128), f),
        ("in_g", (2, 2, 32, 128), f),
        ("pay_k", (2, 8, 128), f),
        ("in_k", (2, 2, 8, 128), f),
        ("ret_s", (2, 2, 48, SL), b),
        ("ret_s_in", (2, 2, 48, SL), b),
        ("ret_g", (2, 2, 8, SL), f),
        ("ret_g_in", (2, 2, 8, SL), f),
        ("ret_a", (2, 2, 16, 256), f),
        ("ret_a_in", (2, 2, 16, 256), f),
        ("pay_dg", (2, 32, 128), f),
        ("in_dg", (2, 4, 32, 128), f),
        ("pay_dk", (2, 8, 128), f),
        ("in_dk", (2, 4, 8, 128), f),
        ("tmp32", (32, 128), f),
        ("tmp8", (8, 128), f),
        ("g32", (GROWS, 128), f),
        ("gb", (2, 4, 8, 16, 128), b),
        ("r1", (4, 8, 16, 128), b),
        ("h1", (4, 8, 16, 128), b),
        ("r2", (3, 8, 16, 128), b),
        ("h2", (8, 16, 128), b),
        ("r3", (4, 8, 16, 128), b),
        ("h3", (8, 16, 128), b),
        ("r4", (4, 8, 16, 128), b),
        ("gout", (2, 4, 8, 16, 128), b),
    ]
    return items


def kernel(n, *refs):
    names = INPUTS + OUTPUTS + tuple(item[0] for item in scratch_list()) + ("ssem", "rsem")
    r = Names(names, refs)
    me = lax.axis_index("tile")
    core = lax.rem(me, 2)
    yy = lax.rem(me // 2, 4)
    nx = min(4, n // 8)
    nz = n // (8 * nx)
    xx = lax.rem(me // 8, nx)
    zz = me // (8 * nx)
    first = me == 0
    last = me == n - 1
    low_on = jnp.where(first, 0.0, 1.0).astype(F32)
    up_on = jnp.where(last, 0.0, 1.0).astype(F32)
    last_f = 1.0 - up_on

    def near(off):
        return lax.rem(me + (off + n), n)

    def at(z, x, y, c):
        return ((z * nx + x) * 4 + y) * 2 + c

    peer_core = at(zz, xx, yy, 1 - core)
    peers_y = [at(zz, xx, lax.rem(yy + s, 4), core) for s in (1, 2, 3)]
    peers_x = [at(zz, lax.rem(xx + s, nx), yy, core) for s in range(1, nx)]
    peers_z = [at(lax.rem(zz + s, nz), xx, yy, core) for s in range(1, nz)]

    count = [0]

    def send(src, dst, dev):
        i = count[0]
        count[0] += 1
        copy = pltpu.make_async_remote_copy(
            src_ref=src,
            dst_ref=dst,
            send_sem=r.ssem.at[i],
            recv_sem=r.rsem.at[i],
            device_id=(dev,),
            device_id_type=MESH,
        )
        copy.start()
        return copy

    def wait(copies):
        for copy in copies:
            copy.wait()

    iota8 = lax.broadcasted_iota(jnp.int32, (8, SL), 0)
    iota32 = lax.broadcasted_iota(jnp.int32, (32, SL), 0) // 4

    everyone = [near(off) for off in OFFS] + peers_y + peers_x + peers_z
    barrier = pltpu.get_barrier_semaphore()
    for dev in everyone:
        pl.semaphore_signal(barrier, inc=1, device_id=(dev,), device_id_type=MESH)

    lane = lax.broadcasted_iota(jnp.int32, (1, SL), 1)

    def meta_rows(k_out, k_air, ref, i):
        used = lane < r.counts[0:1, k_out : k_out + 1]
        ref[i, 0:1, :] = r.sea_cells[k_out].astype(F32)
        ref[i, 1:2, :] = jnp.where(used, r.air_share[k_out], 0.0)
        ref[i, 2:3, :] = jnp.where(used, r.sea_share[k_out], 0.0)
        ref[i, 3:4, :] = r.air_cells[k_air].astype(F32)

    r.meta_pay[...] = jnp.zeros_like(r.meta_pay)
    for i, off in enumerate(OFFS):
        meta_rows(off + 2, 2 - off, r.meta_pay, i)

    for row in range(8):
        lanes = slice(row * 128, (row + 1) * 128)
        r.a_now[:, lanes] = r.air_state[:, row, :]
        r.air_cot[0:8, lanes] = r.air_c[:, row, :]
        r.pay_f[0, row * 4 : row * 4 + 4, :] = r.flux[:, row, :]
    r.air_cot[8:16, :] = jnp.zeros((8, SL), F32)
    for row in range(2):
        lanes = slice(row * 512, (row + 1) * 512)
        r.o_now[:, lanes] = r.sea_state[:, row, :]
        r.sea_cot[:, lanes] = r.sea_c[:, row, :]
        r.wetf[:, lanes] = r.wet[row : row + 1, :].astype(F32)

    def start_f(step):
        return [send(r.pay_f.at[step], r.in_f.at[step, i], near(off)) for i, off in enumerate(OFFS)]

    def start_s(step):
        for hi in range(8):
            r.pay_s[step, hi : hi + 1, :] = r.o_now[0:1, hi * 128 : (hi + 1) * 128]
        return [send(r.pay_s.at[step], r.in_s.at[step, i], near(off)) for i, off in enumerate(OFFS)]

    def start_halo_sea(step):
        r.halo_s[step] = r.o_now[...].astype(BF)
        return [
            send(r.halo_s.at[step], r.halo_s_in.at[step, i], near(off))
            for i, off in enumerate((-1, 1))
        ]

    def start_halo_air(step):
        r.halo_a[step, 0] = r.a_now[:, 0:256]
        r.halo_a[step, 1] = r.a_now[:, SL - 256 : SL]
        return [
            send(r.halo_a.at[step, i], r.halo_a_in.at[step, i], near(off))
            for i, off in enumerate((-1, 1))
        ]

    pl.semaphore_wait(barrier, len(everyone))
    metas = [
        send(r.meta_pay.at[i], r.meta_in.at[off + 2], near(off)) for i, off in enumerate(OFFS)
    ]
    sent_s, sent_f = start_s(0), start_f(0)
    halo_air, halo_sea = start_halo_air(0), start_halo_sea(0)
    meta_rows(2, 2, r.meta_in, 2)

    r.g32[...] = jnp.zeros_like(r.g32)
    for m in (AIR, SEA):
        x = getattr(r, m.name + "_x")
        x[m.state : m.chans, :] = jnp.zeros((m.chans - m.state, m.ext), F32)
        dfs = getattr(r, m.name + "_dfs")
        dfs[...] = jnp.zeros_like(dfs)
        g = lambda s: getattr(r, m.name + "_" + s)
        kc, chans = m.chans, m.inputs
        g("encf")[...] = jnp.zeros_like(g("encf"))
        raw = g("renc")[...].astype(F32)
        for i in range(3):
            for j in range(3):
                t = 3 * i + j
                g("encf")[i * 64 : (i + 1) * 64, j * kc : j * kc + chans] = raw[:, t * chans : (t + 1) * chans]
        enc = g("encf")[...]
        g("enc")[...] = enc.astype(BF)
        g("enct")[...] = jnp.transpose(enc).astype(BF)
        g("exp")[...] = jnp.transpose(g("expt")[...].astype(F32)).astype(BF)
        g("cont")[...] = jnp.transpose(g("con")[...].astype(F32)).astype(BF)
        g("decf")[...] = jnp.zeros_like(g("decf"))
        g("decf")[0 : m.given, :] = g("rdec")[...].astype(F32)
        dec = g("decf")[...]
        g("dec")[...] = dec.astype(BF)
        g("dect")[...] = jnp.transpose(dec).astype(BF)
        taps = jnp.concatenate([g("rdw")[...].astype(F32), jnp.zeros((7, 64), F32)], axis=0)
        g("dw")[...] = jnp.transpose(taps)
    source = lax.broadcasted_iota(jnp.int32, (512, 512), 0)
    r.fold[...] = jnp.where(source == r.partner[...], 1.0, 0.0).astype(BF)
    iota128 = lax.broadcasted_iota(jnp.int32, (128, SL), 0)

    def one_hot(row):
        low = jnp.bitwise_and(row, 127)
        return jnp.where(iota128 == low, 1.0, 0.0).astype(BF)

    for k in range(NEAR):
        lanes = slice(k * SL, (k + 1) * SL)
        r.oh_aa[:, lanes] = one_hot(r.air_cells[k])
        r.oh_ss[:, lanes] = one_hot(r.sea_cells[k])

    def air_meta(k, row):
        return r.meta_in[k, row : row + 1, :]

    def sea_meta(k, row):
        return r.meta_in[4 - k, row : row + 1, :]

    def own_weight(k, row):
        share = r.air_share if row == 1 else r.sea_share
        used = lane < r.counts[0:1, k : k + 1]
        return jnp.where(used, share[k], 0.0)

    wait(metas)
    for k in range(NEAR):
        lanes = slice(k * SL, (k + 1) * SL)
        r.oh_as[:, lanes] = one_hot(air_meta(k, 0).astype(jnp.int32))
        r.oh_sa[:, lanes] = one_hot(sea_meta(k, 3).astype(jnp.int32))

    def high(row):
        return jnp.right_shift(row, 7)

    def regrid(field, wide, src_oh, src_cell, dst_oh, dst_cell, weight):
        iota = iota32 if wide else iota8
        total = None
        for k in range(NEAR):
            lanes = slice(k * SL, (k + 1) * SL)
            picked = nn(field(k).astype(BF), src_oh[:, lanes])
            picked = jnp.where(iota == high(src_cell(k)), picked, 0.0)
            if wide:
                value = (picked[0:8] + picked[8:16]) + (picked[16:24] + picked[24:32])
                value = value + pltpu.roll(value, 4, axis=0)
                value = value * weight(k)
                value = jnp.concatenate([value] * 4, axis=0)
            else:
                value = jnp.sum(picked, axis=0, keepdims=True) * weight(k)
            spread = jnp.where(iota == high(dst_cell(k)), value, 0.0).astype(BF)
            part = nt(spread, dst_oh[:, lanes])
            total = part if total is None else total + part
        return total

    def a_air(k):
        return r.air_cells[k]

    def a_sea(k):
        return air_meta(k, 0).astype(jnp.int32)

    def s_sea(k):
        return r.sea_cells[k]

    def s_air(k):
        return sea_meta(k, 3).astype(jnp.int32)

    def field_of(own, arrived, step, by_air):
        def get(k):
            off = k - 2 if by_air else 2 - k
            if off == 0:
                return own[step]
            return arrived[step, OFFS.index(off)]

        return get

    def weights(m):
        g = lambda s: getattr(r, m.name + "_" + s)
        return g

    def stack_taps(m, step, rows, channels):
        g = weights(m)
        w, kc = m.width, m.chans
        lo, hi = channels
        for row in rows:
            lanes = slice(row * w, (row + 1) * w)
            x = g("x")[lo:hi, lanes]
            g("s3")[step, lo:hi, lanes] = roll(x, 1).astype(BF)
            g("s3")[step, kc + lo : kc + hi, lanes] = x.astype(BF)
            g("s3")[step, 2 * kc + lo : 2 * kc + hi, lanes] = roll(x, -1).astype(BF)

    def forward(m, step):
        g = weights(m)
        w, rows = m.width, m.rows
        enc = g("enc")[...]
        for row in range(rows + 4):
            lanes = slice(row * w, (row + 1) * w)
            g("y")[:, lanes] = nn(enc, g("s3")[step, :, lanes])
        fp, y = g("fp"), g("y")
        for q in list(range(rows + 2)):
            feat = y[0:64, q * w : (q + 1) * w]
            feat = feat + y[64:128, (q + 1) * w : (q + 2) * w]
            feat = feat + y[128:192, (q + 2) * w : (q + 3) * w]
            feat = feat.astype(BF).astype(F32)
            if q == 0:
                feat = feat * low_on
            if q == rows + 1:
                feat = feat * up_on
                if m is SEA:
                    below = fp[step, :, rows * w : (rows + 1) * w].astype(BF)
                    feat = feat + last_f * nn(below, r.fold[...])
            fp[step, :, q * w : (q + 1) * w] = feat
        dw = g("dw")[...]
        for row in range(rows):
            mixed = []
            for j in range(3):
                part = None
                for i in range(3):
                    term = dw[:, 3 * i + j : 3 * i + j + 1] * fp[step, :, (row + i) * w : (row + i + 1) * w]
                    part = term if part is None else part + term
                mixed.append(part)
            g("mix")[:, row * w : (row + 1) * w] = mixed[1] + roll(mixed[0], 1) + roll(mixed[2], -1)
        expand, contract, decoder = g("exp")[...], g("con")[...], g("dec")[...]

        def chunk(c, carry):
            lanes = pl.ds(pl.multiple_of(c * 256, 256), 256)
            own = pl.ds(pl.multiple_of(c * 256 + w, 128), 256)
            x = g("mix")[:, lanes]
            x = x - jnp.mean(x, axis=0, keepdims=True)
            rstd = lax.rsqrt(jnp.mean(x * x, axis=0, keepdims=True) + 1e-06)
            x = x * rstd
            g("nrm")[step, :, lanes] = x
            g("rstd")[step, :, lanes] = rstd
            v = nn(expand, x.astype(BF))
            u = v * v
            t = jnp.tanh(v * (C0 + (C0 * C1) * u))
            half = 0.5 + 0.5 * t
            g("dgelu")[step, :, lanes] = half + (0.5 * v) * (1.0 - t * t) * (C0 + (3.0 * C0 * C1) * u)
            hid = (v * half).astype(BF)
            g("hid")[step, :, lanes] = hid
            res = (fp[step, :, own] + nn(contract, hid)).astype(BF)
            g("resb")[step, :, lanes] = res
            g("out")[:, lanes] = nn(decoder, res)
            return carry

        lax.fori_loop(0, SL // 256, chunk, 0)

    def backward(m, step):
        g = weights(m)
        w, rows = m.width, m.rows
        decoder_t, contract_t, expand_t = g("dect")[...], g("cont")[...], g("expt")[...]

        def chunk(c, carry):
            lanes = pl.ds(pl.multiple_of(c * 256, 256), 256)
            dy = g("cot")[:, lanes]
            if m is SEA:
                dy = dy * r.wetf[:, lanes]
            dy = dy.astype(BF)
            g("dyb")[:, lanes] = dy
            dres = nn(decoder_t, dy).astype(BF)
            g("dresb")[:, lanes] = dres
            dhid = nn(contract_t, dres)
            dpre = (dhid * g("dgelu")[step, :, lanes]).astype(BF)
            g("dpreb")[:, lanes] = dpre
            dn = nn(expand_t, dpre)
            x = g("nrm")[step, :, lanes]
            dmean = jnp.mean(dn, axis=0, keepdims=True)
            dproj = jnp.mean(dn * x, axis=0, keepdims=True)
            g("dmr")[1, :, lanes] = g("rstd")[step, :, lanes] * (dn - dmean - x * dproj)
            return carry

        lax.fori_loop(0, SL // 256, chunk, 0)
        fp, dmr = g("fp"), g("dmr")
        dw = g("dw")[...]
        for row in range(rows):
            lanes = slice(row * w, (row + 1) * w)
            d = dmr[1, :, lanes]
            dmr[0, :, lanes] = roll(d, -1)
            dmr[2, :, lanes] = roll(d, 1)
        spare = None
        for q in range(rows + 1, -1, -1):
            total = None
            for i in range(3):
                row = q - i
                if 0 <= row < rows:
                    for j in range(3):
                        term = dw[:, 3 * i + j : 3 * i + j + 1] * dmr[j, :, row * w : (row + 1) * w]
                        total = term if total is None else total + term
            if 1 <= q <= rows:
                total = total + g("dresb")[:, (q - 1) * w : q * w].astype(F32)
            if q == rows + 1:
                if m is SEA:
                    spare = last_f * nt(total.astype(BF), r.fold[...])
                total = total * up_on
            if q == rows and m is SEA:
                total = total + spare
            if q == 0:
                total = total * low_on
            total = total.astype(BF)
            for i in range(3):
                g("dfs")[i * 64 : (i + 1) * 64, (q + i) * w : (q + i + 1) * w] = total
        enc_t = g("enct")[...]
        kc = m.chans
        for row in range(rows + 4):
            lanes = slice(row * w, (row + 1) * w)
            d = nn(enc_t, g("dfs")[:, lanes])
            g("dx")[:, lanes] = d[kc : 2 * kc] + roll(d[0:kc], -1) + roll(d[2 * kc : 3 * kc], 1)

    def weight_grads(m, step):
        g = weights(m)
        w, rows = m.width, m.rows
        row0 = 0 if m is SEA else 64
        fp, dmr = g("fp"), g("dmr")
        exp = nt(g("nrm")[step].astype(BF), g("dpreb")[...])
        for half in range(2):
            start = G_EXP + 2 * row0 + half * 64
            r.g32[start : start + 64, :] += exp[:, half * 128 : (half + 1) * 128]
        con = nt(g("dresb")[...], g("hid")[step])
        for half in range(2):
            start = G_CON + 2 * row0 + half * 64
            r.g32[start : start + 64, :] += con[:, half * 128 : (half + 1) * 128]
        dec = nt(g("dyb")[...], g("resb")[step])
        start = G_DEC + (0 if m is SEA else 48)
        r.g32[start : start + m.outs, 0:64] += dec
        enc = nt(g("dfs")[...], g("s3")[step])
        if m is SEA:
            r.g32[G_ENC0 : G_ENC0 + 192, :] += enc[:, 0:128]
            r.g32[G_ENC1 : G_ENC1 + 192, 0:64] += enc[:, 128:192]
        else:
            r.g32[G_ENC1 : G_ENC1 + 192, 64 : 64 + 48] += enc
        for i in range(3):
            for j in range(3):
                total = None
                for row in range(rows):
                    term = dmr[j, :, row * w : (row + 1) * w] * fp[step, :, (row + i) * w : (row + i + 1) * w]
                    total = term if total is None else total + term
                t = 3 * i + j + (0 if m is SEA else 16)
                r.g32[G_DW : G_DW + 64, t : t + 1] += jnp.sum(total, axis=1, keepdims=True)

    def regrid_flux(step, sent):
        wait(sent)
        flow = regrid(
            field_of(r.pay_f, r.in_f, step, False), True,
            r.oh_sa, s_air, r.oh_ss, s_sea, lambda k: own_weight(k, 2),
        )
        r.pay_g[step] = flow
        sent = [
            send(r.pay_g.at[step], r.in_g.at[step, i], near(off)) for i, off in enumerate((-1, 1))
        ]
        for hi in range(8):
            r.sea_x[48:52, SL + hi * 128 : SL + (hi + 1) * 128] = r.pay_g[step, hi * 4 : hi * 4 + 4, :]
        return sent

    def regrid_surface(step, sent):
        wait(sent)
        skin = regrid(
            field_of(r.pay_s, r.in_s, step, True), False,
            r.oh_as, a_sea, r.oh_aa, a_air, lambda k: air_meta(k, 1),
        )
        r.pay_k[step] = skin
        sent = [
            send(r.pay_k.at[step], r.in_k.at[step, i], near(off)) for i, off in enumerate((-1, 1))
        ]
        for hi in range(8):
            r.air_x[8:9, 256 + hi * 128 : 256 + (hi + 1) * 128] = r.pay_k[step, hi : hi + 1, :]
        return sent

    def sea_states(step, sent):
        r.sea_x[0:48, SL : 2 * SL] = r.halo_s[step].astype(F32)
        wait(sent)
        r.sea_x[0:48, 0:SL] = r.halo_s_in[step, 1].astype(F32) * low_on
        r.sea_x[0:48, 2 * SL : 3 * SL] = r.halo_s_in[step, 0].astype(F32) * up_on
        folded = nn(r.halo_s[step, :, 512:SL], r.fold[...])
        r.sea_x[0:48, 2 * SL : 2 * SL + 512] += last_f * folded
        stack_taps(SEA, step, range(6), (0, 48))

    def sea_forward(step, sent):
        wait(sent)
        for hi in range(8):
            r.sea_x[48:52, hi * 128 : (hi + 1) * 128] = r.in_g[step, 1, hi * 4 : hi * 4 + 4, :] * low_on
            r.sea_x[48:52, 2 * SL + hi * 128 : 2 * SL + (hi + 1) * 128] = (
                r.in_g[step, 0, hi * 4 : hi * 4 + 4, :] * up_on
            )
        folded = nn(r.sea_x[48:64, SL + 512 : 2 * SL].astype(BF), r.fold[...])
        r.sea_x[48:64, 2 * SL : 2 * SL + 512] += last_f * folded
        stack_taps(SEA, step, range(6), (48, 64))
        forward(SEA, step)
        r.o_now[...] += r.wetf[...] * r.sea_out[...]

    def air_states(step, sent):
        r.air_x[0:8, 256 : 256 + SL] = r.a_now[...]
        wait(sent)
        r.air_x[0:8, 0:256] = r.halo_a_in[step, 1] * low_on
        r.air_x[0:8, 256 + SL : 512 + SL] = r.halo_a_in[step, 0] * up_on

    def air_forward(step, sent):
        wait(sent)
        for i in range(2):
            r.air_x[8:9, i * 128 : (i + 1) * 128] = r.in_k[step, 1, 6 + i : 7 + i, :] * low_on
            r.air_x[8:9, 256 + SL + i * 128 : 256 + SL + (i + 1) * 128] = (
                r.in_k[step, 0, i : i + 1, :] * up_on
            )
        stack_taps(AIR, step, range(12), (0, 16))
        forward(AIR, step)
        r.a_now[...] += r.air_out[0:8, :]

    def start_c_sea(step):
        copies = []
        for i, off in enumerate((-1, 1)):
            lanes = slice(i * 2 * SL, i * 2 * SL + SL)
            r.ret_g[step, i] = r.sea_dx[48:56, lanes]
            copies.append(send(r.ret_g.at[step, i], r.ret_g_in.at[step, i], near(off)))
        for i, off in enumerate((-1, 1)):
            lanes = slice(i * 2 * SL, i * 2 * SL + SL)
            r.ret_s[step, i] = r.sea_dx[0:48, lanes].astype(BF)
            copies.append(send(r.ret_s.at[step, i], r.ret_s_in.at[step, i], near(off)))
        back = nt(r.sea_dx[:, 2 * SL : 2 * SL + 512].astype(BF), r.fold[...])
        r.sea_dx[:, SL + 512 : 2 * SL] += last_f * back
        return copies

    def start_c_air(step):
        copies = []
        for i, off in enumerate((-1, 1)):
            start = i * (256 + SL)
            r.ret_a[step, i] = r.air_dx[:, start : start + 256]
            copies.append(send(r.ret_a.at[step, i], r.ret_a_in.at[step, i], near(off)))
        return copies

    def start_dg(step, sent):
        wait(sent[0:2])
        own = slice(SL, 2 * SL)
        r.sea_dx[48:56, own] += r.ret_g_in[step, 1] * low_on + r.ret_g_in[step, 0] * up_on
        for hi in range(8):
            r.pay_dg[step, hi * 4 : hi * 4 + 4, :] = r.sea_dx[48:52, SL + hi * 128 : SL + (hi + 1) * 128]
        return [send(r.pay_dg.at[step], r.in_dg.at[step, i], near(off)) for i, off in enumerate(OFFS)]

    def start_dk(step, sent):
        wait(sent)
        own = slice(256, 512)
        r.air_dx[:, own] += r.ret_a_in[step, 1] * low_on
        own = slice(SL, SL + 256)
        r.air_dx[:, own] += r.ret_a_in[step, 0] * up_on
        for hi in range(8):
            r.pay_dk[step, hi : hi + 1, :] = r.air_dx[8:9, 256 + hi * 128 : 256 + (hi + 1) * 128]
        sent = [send(r.pay_dk.at[step], r.in_dk.at[step, i], near(off)) for i, off in enumerate(OFFS)]
        r.air_cot[0:8, :] += r.air_dx[0:8, 256 : 256 + SL]
        return sent

    def finish_sea_cot(step, sent):
        wait(sent[2:4])
        r.sea_cot[...] += (
            r.sea_dx[0:48, SL : 2 * SL]
            + r.ret_s_in[step, 1].astype(F32) * low_on
            + r.ret_s_in[step, 0].astype(F32) * up_on
        )

    def finish_dg(step, sent):
        wait(sent)
        r.tmp32[...] = regrid(
            field_of(r.pay_dg, r.in_dg, step, True), True,
            r.oh_as, a_sea, r.oh_aa, a_air, lambda k: air_meta(k, 2),
        )
        for hi in range(8):
            r.air_cot[8:12, hi * 128 : (hi + 1) * 128] = r.tmp32[hi * 4 : hi * 4 + 4, :]

    def finish_dk(step, sent):
        wait(sent)
        r.tmp8[...] = regrid(
            field_of(r.pay_dk, r.in_dk, step, False), False,
            r.oh_sa, s_air, r.oh_ss, s_sea, lambda k: own_weight(k, 1),
        )
        for hi in range(8):
            r.sea_cot[0:1, hi * 128 : (hi + 1) * 128] += r.tmp8[hi : hi + 1, :]

    sent_k = regrid_surface(0, sent_s)
    sent_g = regrid_flux(0, sent_f)
    air_states(0, halo_air)
    sea_states(0, halo_sea)
    air_forward(0, sent_k)
    for hi in range(8):
        r.pay_f[1, hi * 4 : hi * 4 + 4, :] = r.air_out[8:12, hi * 128 : (hi + 1) * 128]
    sent_f = start_f(1)
    halo_air = start_halo_air(1)
    sea_forward(0, sent_g)
    sent_s = start_s(1)
    halo_sea = start_halo_sea(1)

    air_states(1, halo_air)
    sent_g = regrid_flux(1, sent_f)
    sea_states(1, halo_sea)
    sent_k = regrid_surface(1, sent_s)
    sea_forward(1, sent_g)
    backward(SEA, 1)
    sea_c = start_c_sea(1)
    for row in range(2):
        r.o_sea[:, row, :] = r.o_now[:, row * 512 : (row + 1) * 512]
    air_forward(1, sent_k)
    backward(AIR, 1)
    air_c = start_c_air(1)
    for row in range(8):
        r.o_air[:, row, :] = r.a_now[:, row * 128 : (row + 1) * 128]

    weight_grads(SEA, 1)
    sent_dg = start_dg(1, sea_c)
    weight_grads(AIR, 1)
    finish_sea_cot(1, sea_c)
    sent_dk = start_dk(1, air_c)
    finish_dg(1, sent_dg)
    backward(AIR, 0)
    air_c = start_c_air(0)
    weight_grads(AIR, 0)
    finish_dk(1, sent_dk)
    backward(SEA, 0)
    sea_c = start_c_sea(0)
    weight_grads(SEA, 0)

    for c in range(2):
        for y in range(4):
            for e in range(8):
                start = ((c * 4 + y) * 8 + e) * 16
                r.gb[c, y, e] = r.g32[start : start + 16, :].astype(BF)
    sum_core = [send(r.gb.at[1 - core], r.r1, peer_core)]
    sent_dk = start_dk(0, air_c)
    wait(sum_core)
    r.h1[...] = (r.gb[core].astype(F32) + r.r1[...].astype(F32)).astype(BF)
    sum_y = [
        send(r.h1.at[lax.rem(yy + s, 4)], r.r2.at[s - 1], peers_y[s - 1]) for s in (1, 2, 3)
    ]
    for row in range(8):
        r.o_dair[:, row, :] = r.air_cot[0:8, row * 128 : (row + 1) * 128]
    sent_dg = start_dg(0, sea_c)
    wait(sum_y)
    h2 = r.h1[yy].astype(F32)
    for s in range(3):
        h2 = h2 + r.r2[s].astype(F32)
    h2 = h2.astype(BF)
    r.h2[...] = h2
    r.r3[xx] = h2
    sum_x = [send(r.h2, r.r3.at[xx], dev) for dev in peers_x]
    finish_sea_cot(0, sea_c)
    finish_dk(0, sent_dk)
    for row in range(2):
        r.o_dsea[:, row, :] = r.sea_cot[:, row * 512 : (row + 1) * 512]
    wait(sum_x)
    h3 = r.r3[0].astype(F32)
    for s in range(1, nx):
        h3 = h3 + r.r3[s].astype(F32)
    h3 = h3.astype(BF)
    r.h3[...] = h3
    r.r4[zz] = h3
    sum_z = [send(r.h3, r.r4.at[zz], dev) for dev in peers_z]
    finish_dg(0, sent_dg)
    for row in range(8):
        r.o_dflux[:, row, :] = r.air_cot[8:12, row * 128 : (row + 1) * 128]
    wait(sum_z)
    h4 = r.r4[0].astype(F32)
    for s in range(1, nz):
        h4 = h4 + r.r4[s].astype(F32)
    r.gout[core, yy] = h4.astype(BF)
    give_y = [send(r.gout.at[core, yy], r.gout.at[core, yy], dev) for dev in peers_y]
    wait(give_y)
    give_core = [send(r.gout.at[core], r.gout.at[core], peer_core)]
    wait(give_core)
    r.o_grads[...] = r.gout[...]


def finish(n, *refs):
    given, results = refs[0:5], refs[6:11]
    r = Names(
        ("grads",) + tuple("o_" + m + "_" + w for m in ("air", "sea") for w in WEIGHTS) + ("g32",),
        (refs[5],) + refs[11:],
    )
    for a, b in zip(given, results):
        b[...] = a[...]
    for c in range(2):
        for y in range(4):
            for e in range(8):
                start = ((c * 4 + y) * 8 + e) * 16
                r.g32[start : start + 16, :] = r.grads[c, y, e].astype(F32)

    scale = 1.0 / math.sqrt(SL * n)
    for m in (AIR, SEA):
        o = lambda s: getattr(r, "o_" + m.name + "_" + s)
        col = 0 if m is SEA else 64
        for half in range(2):
            start = G_EXP + 2 * col + half * 64
            o("exp")[:, half * 128 : (half + 1) * 128] = r.g32[start : start + 64, :] * scale
            start = G_CON + 2 * col + half * 64
            o("con")[:, half * 128 : (half + 1) * 128] = r.g32[start : start + 64, :] * scale
        start = G_DEC + (0 if m is SEA else 48)
        count_out = 48 if m is SEA else 12
        o("dec")[...] = r.g32[start : start + count_out, 0:64] * scale
        shift = 0 if m is SEA else 16
        o("dw")[...] = (jnp.transpose(r.g32[G_DW : G_DW + 64, :]) * scale)[shift : shift + 9, :]
        chans = 52 if m is SEA else 9
        for i in range(3):
            for j in range(3):
                t = 3 * i + j
                if m is AIR:
                    base, left = G_ENC1, 64 + 16 * j
                else:
                    base, left = (G_ENC0, 64 * j) if j < 2 else (G_ENC1, 0)
                piece = r.g32[base + i * 64 : base + (i + 1) * 64, left : left + chans]
                o("enc")[:, t * chans : (t + 1) * chans] = piece * scale


def body(n, *args):
    (
        air_state, sea_state, flux, air_cells, sea_cells, counts, sea_share, air_share, partner, wet,
        air_c, sea_c, air_enc, air_dw, air_exp, air_con, air_dec, sea_enc, sea_dw, sea_exp, sea_con,
        sea_dec,
    ) = args
    slots = lambda x: jnp.transpose(x, (1, 0, 2))
    given = [
        air_state, sea_state, flux, slots(air_cells), slots(sea_cells), counts, slots(sea_share),
        slots(air_share), partner[None], wet, air_c, sea_c,
        air_enc, air_dw.T, air_exp.T, air_con, air_dec, sea_enc, sea_dw.T, sea_exp.T, sea_con, sea_dec,
    ]
    vmem = pl.BlockSpec(memory_space=pltpu.VMEM)
    fields = [jax.ShapeDtypeStruct(x.shape, F32) for x in (air_state, sea_state, air_c, sea_c, flux)]
    made = pl.pallas_call(
        lambda *refs: kernel(n, *refs),
        out_shape=fields + [jax.ShapeDtypeStruct((2, 4, 8, 16, 128), BF)],
        in_specs=[vmem] * len(given),
        out_specs=[vmem] * 6,
        scratch_shapes=[pltpu.VMEM(shape, kind) for _, shape, kind in scratch_list()]
        + [pltpu.SemaphoreType.DMA((COPIES,)), pltpu.SemaphoreType.DMA((COPIES,))],
        compiler_params=pltpu.CompilerParams(
            collective_id=0, has_side_effects=True, vmem_limit_bytes=60 * 1024 * 1024
        ),
        name="coupled",
    )(*given)
    grads = [air_enc, air_dw.T, air_exp.T, air_con, air_dec, sea_enc, sea_dw.T, sea_exp.T, sea_con, sea_dec]
    done = pl.pallas_call(
        lambda *refs: finish(n, *refs),
        out_shape=fields + [jax.ShapeDtypeStruct(x.shape, F32) for x in grads],
        in_specs=[vmem] * 6,
        out_specs=[vmem] * 15,
        scratch_shapes=[pltpu.VMEM((GROWS, 128), F32)],
        name="finish",
    )(*made)
    done = list(done)
    for i in (6, 7, 11, 12):
        done[i] = done[i].T
    return done


def solution(mesh):
    n = mesh.shape["tile"]
    rows = P(None, "tile", None)
    slots = P("tile", None, None)
    return jax.shard_map(
        lambda *args: tuple(body(n, *args)),
        mesh=mesh,
        in_specs=(rows, rows, rows, slots, slots, P("tile", None), slots, slots, P(), P("tile", None), rows, rows)
        + (P(),) * 10,
        out_specs=(rows,) * 5 + (P(),) * 10,
        check_vma=False,
    )
```

```python
import math

import jax
import jax.numpy as jnp
from jax import lax
from jax.experimental import pallas as pl
from jax.experimental.pallas import tpu as pltpu
from jax.sharding import PartitionSpec as P

MESH = pl.DeviceIdType.MESH
F32 = jnp.float32
BF = jnp.bfloat16
OFFS = (-2, -1, 1, 2)
AROUND = (-2, -1, 0, 1, 2)
NEAR = 5
SL = 1024
C0 = math.sqrt(2.0 / math.pi)
C1 = 0.044715


def nn(a, b):
    return jnp.dot(a, b, preferred_element_type=F32)


def nt(a, b):
    return lax.dot_general(a, b, (((1,), (1,)), ((), ())), preferred_element_type=F32)


def tn(a, b):
    return lax.dot_general(a, b, (((0,), (0,)), ((), ())), preferred_element_type=F32)


def roll(x, by):
    return pltpu.roll(x, by % x.shape[1], axis=1)


def at_band(z, xr, y, core, nx, flip):
    return ((z * nx + xr) * 4 + flip(y, 4, lax.rem(xr, 2))) * 2 + core


class Either:
    def __init__(self, own, local, remote):
        self.own, self.local, self.remote = own, local, remote

    def start(self):
        pl.when(self.own)(self.local.start)
        pl.when(jnp.logical_not(self.own))(self.remote.start)

    def wait(self):
        pl.when(self.own)(self.local.wait)
        pl.when(jnp.logical_not(self.own))(self.remote.wait)


class Names:
    def __init__(self, names, refs):
        for name, ref in zip(names, refs):
            setattr(self, name, ref)


class Model:
    def __init__(self, name, rows, width, state, inputs, chans, given, outs):
        self.name, self.rows, self.width = name, rows, width
        self.state, self.chans, self.outs = state, chans, outs
        self.inputs, self.given = inputs, given
        self.ext = (rows + 4) * width
        self.pad = (rows + 2) * width

    def scratch(self):
        f, b = F32, BF
        n, kc = self.name, self.chans
        return [
            (n + "_x", (kc, self.ext), f),
            (n + "_s3", (2, 3 * kc, self.ext), b),
            (n + "_y", (192, self.ext), f),
            (n + "_fp", (2, 64, self.pad), f),
            (n + "_mix", (64, SL), f),
            (n + "_nrm", (2, 64, SL), f),
            (n + "_rstd", (2, 1, SL), f),
            (n + "_dgelu", (2, 256, SL), f),
            (n + "_hid", (2, 256, SL), b),
            (n + "_resb", (2, 64, SL), b),
            (n + "_out", (self.outs, SL), f),
            (n + "_cot", (self.outs, SL), f),
            (n + "_dyb", (self.outs, SL), b),
            (n + "_dresb", (64, SL), b),
            (n + "_dpreb", (256, SL), b),
            (n + "_dmr", (3, 64, SL), f),
            (n + "_dfs", (192, self.ext), b),
            (n + "_ds3", (3 * kc, self.ext), f),
            (n + "_dx", (kc, self.ext), f),
            (n + "_encf", (192, 3 * kc), f),
            (n + "_enc", (192, 3 * kc), b),
            (n + "_enct", (3 * kc, 192), b),
            (n + "_exp", (256, 64), b),
            (n + "_cont", (256, 64), b),
            (n + "_decf", (self.outs, 64), f),
            (n + "_dec", (self.outs, 64), b),
            (n + "_dect", (64, self.outs), b),
            (n + "_dw", (64, 16), f),
        ]


AIR = Model("air", 8, 128, 8, 9, 16, 12, 16)
SEA = Model("sea", 2, 512, 48, 52, 64, 48, 48)

INPUTS = (
    "air_state",
    "sea_state",
    "flux",
    "air_cells",
    "sea_cells",
    "counts",
    "sea_share",
    "air_share",
    "partner",
    "wet",
    "air_c",
    "sea_c",
    "air_renc",
    "air_rdw",
    "air_expt",
    "air_con",
    "air_rdec",
    "sea_renc",
    "sea_rdw",
    "sea_expt",
    "sea_con",
    "sea_rdec",
)
OUTPUTS = ("o_air", "o_sea", "o_dair", "o_dsea", "o_dflux", "o_grads")
WEIGHTS = ("enc", "dw", "exp", "con", "dec")

COPIES = 96
GROWS = 1024
G_EXP, G_CON, G_ENC0, G_ENC1, G_DEC, G_DW = 0, 256, 512, 704, 896, 960


def scratch_list():
    f, b = F32, BF
    items = AIR.scratch() + SEA.scratch()
    items += [
        ("meta_pay", (4, 4, SL), f),
        ("meta_in", (4, 4, SL), f),
        ("own_f", (32, SL), f),
        ("own_pay", (32, SL), b),
        ("own_in", (32, SL), b),
        ("own", (24, SL), f),
        ("band_a", (8, SL), f),
        ("band_a_in", (8, SL), f),
        ("cots", (48, SL), b),
        ("cots_in", (48, SL), b),
        ("cota", (8, SL), f),
        ("cota_in", (8, SL), f),
        ("home_air", (8, SL), f),
        ("home_sea", (48, SL), b),
        ("back_sea", (48, SL), b),
        ("home_dair", (16, SL), f),
        ("home_dsea", (48, SL), b),
        ("back_dsea", (48, SL), b),
        ("oh_aa", (128, NEAR * SL), b),
        ("oh_as", (128, NEAR * SL), b),
        ("oh_sa", (128, NEAR * SL), b),
        ("oh_ss", (128, NEAR * SL), b),
        ("fold", (512, 512), b),
        ("wetf", (1, SL), f),
        ("a_now", (8, SL), f),
        ("o_now", (48, SL), f),
        ("new_f", (32, 128), f),
        ("pay_f", (2, 32, 128), b),
        ("in_f", (2, 5, 32, 128), b),
        ("pay_s", (2, 8, 128), f),
        ("in_s", (2, 5, 8, 128), f),
        ("halo_s", (2, 48, SL), b),
        ("halo_s_in", (2, 3, 48, SL), b),
        ("halo_a", (2, 2, 8, 256), f),
        ("halo_a_in", (2, 2, 8, 256), f),
        ("pay_g", (2, 32, 128), f),
        ("in_g", (2, 2, 32, 128), f),
        ("pay_k", (2, 8, 128), f),
        ("in_k", (2, 2, 8, 128), f),
        ("ret_s", (2, 2, 48, SL), b),
        ("ret_s_in", (2, 2, 48, SL), b),
        ("ret_g", (2, 2, 8, SL), f),
        ("ret_g_in", (2, 2, 8, SL), f),
        ("ret_a", (2, 2, 16, 256), f),
        ("ret_a_in", (2, 2, 16, 256), f),
        ("pay_dg", (2, 32, 128), f),
        ("in_dg", (2, 4, 32, 128), f),
        ("pay_dk", (2, 8, 128), f),
        ("in_dk", (2, 4, 8, 128), f),
        ("tmp32", (32, 128), f),
        ("tmp8", (8, 128), f),
        ("g32", (GROWS, 128), f),
        ("gb", (2, 4, 8, 16, 128), b),
        ("r1", (4, 8, 16, 128), b),
        ("h1", (4, 8, 16, 128), b),
        ("r2", (3, 8, 16, 128), b),
        ("h2", (8, 16, 128), b),
        ("r3", (4, 8, 16, 128), b),
        ("h3", (8, 16, 128), b),
        ("r4", (4, 8, 16, 128), b),
        ("gout", (2, 4, 8, 16, 128), b),
    ]
    return items


def kernel(n, *refs):
    names = INPUTS + OUTPUTS + tuple(item[0] for item in scratch_list()) + ("ssem", "rsem")
    r = Names(names, refs)
    me = lax.axis_index("tile")
    core = lax.rem(me, 2)
    yy = lax.rem(me // 2, 4)
    nx = min(4, n // 8)
    nz = n // (8 * nx)
    xx = lax.rem(me // 8, nx)
    zz = me // (8 * nx)

    def flip(value, size, odd):
        return value + odd * (size - 1 - 2 * value)

    def worker(band):
        c, chip = lax.rem(band, 2), band // 2
        z, xr, yr = chip // (4 * nx), lax.rem(chip // 4, nx), lax.rem(chip, 4)
        x = flip(xr, nx, lax.rem(z, 2))
        y = flip(yr, 4, lax.rem(xr, 2))
        return ((z * nx + x) * 4 + y) * 2 + c

    band = at_band(zz, flip(xx, nx, lax.rem(zz, 2)), yy, core, nx, flip)
    first = band == 0
    last = band == n - 1
    low_on = jnp.where(first, 0.0, 1.0).astype(F32)
    up_on = jnp.where(last, 0.0, 1.0).astype(F32)
    last_f = 1.0 - up_on

    def near(off):
        return worker(lax.rem(band + (off + n), n))

    def served(off):
        return worker(lax.rem(me + (off + n), n))

    def at(z, x, y, c):
        return ((z * nx + x) * 4 + y) * 2 + c

    peer_core = at(zz, xx, yy, 1 - core)
    peers_y = [at(zz, xx, lax.rem(yy + s, 4), core) for s in (1, 2, 3)]
    peers_x = [at(zz, lax.rem(xx + s, nx), yy, core) for s in range(1, nx)]
    peers_z = [at(lax.rem(zz + s, nz), xx, yy, core) for s in range(1, nz)]

    count = [0]

    def give(src, dst, dev):
        i = count[0]
        count[0] += 1
        remote = pltpu.make_async_remote_copy(
            src_ref=src,
            dst_ref=dst,
            send_sem=r.ssem.at[i],
            recv_sem=r.rsem.at[i],
            device_id=(dev,),
            device_id_type=MESH,
        )
        copy = Either(dev == me, pltpu.make_async_copy(src, dst, r.rsem.at[i]), remote)
        copy.start()
        return copy

    def send(src, dst, dev):
        i = count[0]
        count[0] += 1
        copy = pltpu.make_async_remote_copy(
            src_ref=src,
            dst_ref=dst,
            send_sem=r.ssem.at[i],
            recv_sem=r.rsem.at[i],
            device_id=(dev,),
            device_id_type=MESH,
        )
        copy.start()
        return copy

    def wait(copies):
        for copy in copies:
            copy.wait()

    iota8 = lax.broadcasted_iota(jnp.int32, (8, SL), 0)
    iota32 = lax.broadcasted_iota(jnp.int32, (32, SL), 0) // 4

    senders = [near(off) for off in OFFS] + peers_y + peers_x + peers_z
    barrier = pltpu.get_barrier_semaphore()
    for dev in senders:
        pl.semaphore_signal(barrier, inc=1, device_id=(dev,), device_id_type=MESH)
    either = [lax.rem(band + (n - off), n) for off in AROUND] + [worker(me)]

    def greet(dev):
        def there():
            pl.semaphore_signal(barrier, inc=1, device_id=(dev,), device_id_type=MESH)

        pl.when(dev != me)(there)

    greetings = len(senders)
    for dev in either:
        greet(dev)
        greetings = greetings + (dev != me).astype(jnp.int32)

    lane = lax.broadcasted_iota(jnp.int32, (1, SL), 1)

    def slot_rows(k_out, k_air, put):
        used = lane < r.counts[0:1, k_out : k_out + 1]
        put(0, r.sea_cells[k_out].astype(F32))
        put(1, jnp.where(used, r.air_share[k_out], 0.0))
        put(2, jnp.where(used, r.sea_share[k_out], 0.0))
        put(3, r.air_cells[k_air].astype(F32))

    for i, off in enumerate(OFFS):

        def put(row, value, i=i):
            r.meta_pay[i, row : row + 1, :] = value

        slot_rows(off + 2, 2 - off, put)
    for k in range(NEAR):

        def put(row, value, k=k):
            base = 6 * k
            if row in (1, 2):
                r.own_f[base + 3 + row : base + 4 + row, :] = value
            else:
                high = jnp.floor(value * (1.0 / 128.0))
                start = base + (0 if row == 0 else 2)
                r.own_f[start : start + 1, :] = high
                r.own_f[start + 1 : start + 2, :] = value - 128.0 * high

        slot_rows(k, k, put)
    r.own_f[31:32, :] = jnp.zeros((1, SL), F32)
    for row in range(8):
        lanes = slice(row * 128, (row + 1) * 128)
        r.band_a[:, lanes] = r.air_state[:, row, :]
        r.cota[:, lanes] = r.air_c[:, row, :]
        r.new_f[row * 4 : row * 4 + 4, :] = r.flux[:, row, :]
    for row in range(2):
        lanes = slice(row * 512, (row + 1) * 512)
        r.halo_s[0, :, lanes] = r.sea_state[:, row, :].astype(BF)
        r.own_f[30:31, lanes] = r.wet[row : row + 1, :].astype(F32)
    for hi in range(8):
        row, left = hi // 4, (hi % 4) * 128
        r.pay_s[0, hi : hi + 1, :] = r.sea_state[0, row : row + 1, left : left + 128]
    r.pay_f[0] = r.new_f[...].astype(BF)
    r.own_pay[...] = r.own_f[...].astype(BF)
    r.halo_a[0, 0] = r.band_a[:, 0:256]
    r.halo_a[0, 1] = r.band_a[:, SL - 256 : SL]

    def start_f(step):
        return [send(r.pay_f.at[step], r.in_f.at[step, off + 2], near(off)) for off in OFFS]

    def start_s(step):
        for hi in range(8):
            r.pay_s[step, hi : hi + 1, :] = r.o_now[0:1, hi * 128 : (hi + 1) * 128]
        return [send(r.pay_s.at[step], r.in_s.at[step, off + 2], near(off)) for off in OFFS]

    def start_halo_sea(step):
        r.halo_s[step] = r.o_now[...].astype(BF)
        return [
            send(r.halo_s.at[step], r.halo_s_in.at[step, off + 1], near(off))
            for off in (-1, 1)
        ]

    def start_halo_air(step):
        r.halo_a[step, 0] = r.a_now[:, 0:256]
        r.halo_a[step, 1] = r.a_now[:, SL - 256 : SL]
        return [
            send(r.halo_a.at[step, i], r.halo_a_in.at[step, i], near(off))
            for i, off in enumerate((-1, 1))
        ]

    pl.semaphore_wait(barrier, greetings)
    metas = [give(r.own_pay, r.own_in, served(0))]
    for i, off in enumerate(OFFS):
        metas.append(give(r.meta_pay.at[i], r.meta_in.at[i], served(off)))
    sent_s = [give(r.pay_s.at[0], r.in_s.at[0, off + 2], served(off)) for off in AROUND]
    sent_f = [give(r.pay_f.at[0], r.in_f.at[0, off + 2], served(off)) for off in AROUND]
    halo_air = [give(r.band_a, r.band_a_in, served(0))]
    for i, off in enumerate((-1, 1)):
        halo_air.append(give(r.halo_a.at[0, i], r.halo_a_in.at[0, i], served(off)))
    own_sea = [give(r.halo_s.at[0], r.halo_s_in.at[0, 1], served(0))]
    for row in range(2):
        lanes = slice(row * 512, (row + 1) * 512)
        r.cots[:, lanes] = r.sea_c[:, row, :].astype(BF)

    r.g32[...] = jnp.zeros_like(r.g32)
    for m in (AIR, SEA):
        x = getattr(r, m.name + "_x")
        x[m.state : m.chans, :] = jnp.zeros((m.chans - m.state, m.ext), F32)
        dfs = getattr(r, m.name + "_dfs")
        dfs[...] = jnp.zeros_like(dfs)
        g = lambda s: getattr(r, m.name + "_" + s)
        kc, chans = m.chans, m.inputs
        g("encf")[...] = jnp.zeros_like(g("encf"))
        raw = g("renc")[...].astype(F32)
        for i in range(3):
            for j in range(3):
                t = 3 * i + j
                g("encf")[i * 64 : (i + 1) * 64, j * kc : j * kc + chans] = raw[:, t * chans : (t + 1) * chans]
        enc = g("encf")[...]
        g("enc")[...] = enc.astype(BF)
        g("enct")[...] = jnp.transpose(enc).astype(BF)
        g("exp")[...] = jnp.transpose(g("expt")[...].astype(F32)).astype(BF)
        g("cont")[...] = jnp.transpose(g("con")[...].astype(F32)).astype(BF)
        g("decf")[...] = jnp.zeros_like(g("decf"))
        g("decf")[0 : m.given, :] = g("rdec")[...].astype(F32)
        dec = g("decf")[...]
        g("dec")[...] = dec.astype(BF)
        g("dect")[...] = jnp.transpose(dec).astype(BF)
        taps = jnp.concatenate([g("rdw")[...].astype(F32), jnp.zeros((7, 64), F32)], axis=0)
        g("dw")[...] = jnp.transpose(taps)
    source = lax.broadcasted_iota(jnp.int32, (512, 512), 0)
    r.fold[...] = jnp.where(source == r.partner[...], 1.0, 0.0).astype(BF)
    iota128 = lax.broadcasted_iota(jnp.int32, (128, SL), 0)

    def one_hot(row):
        low = jnp.bitwise_and(row, 127)
        return jnp.where(iota128 == low, 1.0, 0.0).astype(BF)

    def own_row(k, row):
        return r.own[4 * k + row : 4 * k + row + 1, :]

    def air_meta(k, row):
        if k == 2:
            return own_row(2, row)
        return r.meta_in[OFFS.index(k - 2), row : row + 1, :]

    def sea_meta(k, row):
        return air_meta(4 - k, row)

    def own_weight(k, row):
        return own_row(k, row)

    def a_air(k):
        return own_row(k, 3).astype(jnp.int32)

    def a_sea(k):
        return air_meta(k, 0).astype(jnp.int32)

    def s_sea(k):
        return own_row(k, 0).astype(jnp.int32)

    def s_air(k):
        return sea_meta(k, 3).astype(jnp.int32)

    wait(metas)
    arrived = r.own_in[...].astype(F32)
    for k in range(NEAR):
        base = 6 * k
        r.own[4 * k : 4 * k + 1, :] = arrived[base : base + 1] * 128.0 + arrived[base + 1 : base + 2]
        r.own[4 * k + 1 : 4 * k + 3, :] = arrived[base + 4 : base + 6]
        r.own[4 * k + 3 : 4 * k + 4, :] = arrived[base + 2 : base + 3] * 128.0 + arrived[base + 3 : base + 4]
    r.wetf[...] = arrived[30:31]
    for k in range(NEAR):
        lanes = slice(k * SL, (k + 1) * SL)
        r.oh_aa[:, lanes] = one_hot(a_air(k))
        r.oh_ss[:, lanes] = one_hot(s_sea(k))
        r.oh_as[:, lanes] = one_hot(a_sea(k))
        r.oh_sa[:, lanes] = one_hot(s_air(k))

    def high(row):
        return jnp.right_shift(row, 7)

    def regrid(field, wide, src_oh, src_cell, dst_oh, dst_cell, weight):
        iota = iota32 if wide else iota8
        total = None
        for k in range(NEAR):
            lanes = slice(k * SL, (k + 1) * SL)
            picked = nn(field(k).astype(BF), src_oh[:, lanes])
            picked = jnp.where(iota == high(src_cell(k)), picked, 0.0)
            if wide:
                value = (picked[0:8] + picked[8:16]) + (picked[16:24] + picked[24:32])
                value = value + pltpu.roll(value, 4, axis=0)
                value = value * weight(k)
                value = jnp.concatenate([value] * 4, axis=0)
            else:
                value = jnp.sum(picked, axis=0, keepdims=True) * weight(k)
            spread = jnp.where(iota == high(dst_cell(k)), value, 0.0).astype(BF)
            part = nt(spread, dst_oh[:, lanes])
            total = part if total is None else total + part
        return total

    def field_of(own, arrived, step, by_air):
        def get(k):
            off = k - 2 if by_air else 2 - k
            if off == 0 and not (arrived.shape[1] == NEAR and step == 0):
                return own[step]
            return arrived[step, (AROUND if arrived.shape[1] == NEAR else OFFS).index(off)]

        return get

    def weights(m):
        g = lambda s: getattr(r, m.name + "_" + s)
        return g

    def stack_taps(m, step, rows, channels):
        g = weights(m)
        w, kc = m.width, m.chans
        lo, hi = channels
        for row in rows:
            lanes = slice(row * w, (row + 1) * w)
            x = g("x")[lo:hi, lanes]
            g("s3")[step, lo:hi, lanes] = roll(x, 1).astype(BF)
            g("s3")[step, kc + lo : kc + hi, lanes] = x.astype(BF)
            g("s3")[step, 2 * kc + lo : 2 * kc + hi, lanes] = roll(x, -1).astype(BF)

    def forward(m, step):
        g = weights(m)
        w, rows = m.width, m.rows
        enc = g("enc")[...]
        for row in range(rows + 4):
            lanes = slice(row * w, (row + 1) * w)
            g("y")[:, lanes] = nn(enc, g("s3")[step, :, lanes])
        fp, y = g("fp"), g("y")
        for q in list(range(rows + 2)):
            feat = y[0:64, q * w : (q + 1) * w]
            feat = feat + y[64:128, (q + 1) * w : (q + 2) * w]
            feat = feat + y[128:192, (q + 2) * w : (q + 3) * w]
            feat = feat.astype(BF).astype(F32)
            if q == 0:
                feat = feat * low_on
            if q == rows + 1:
                feat = feat * up_on
                if m is SEA:
                    below = fp[step, :, rows * w : (rows + 1) * w].astype(BF)
                    feat = feat + last_f * nn(below, r.fold[...])
            fp[step, :, q * w : (q + 1) * w] = feat
        dw = g("dw")[...]
        for row in range(rows):
            mixed = []
            for j in range(3):
                part = None
                for i in range(3):
                    term = dw[:, 3 * i + j : 3 * i + j + 1] * fp[step, :, (row + i) * w : (row + i + 1) * w]
                    part = term if part is None else part + term
                mixed.append(part)
            g("mix")[:, row * w : (row + 1) * w] = mixed[1] + roll(mixed[0], 1) + roll(mixed[2], -1)
        expand, contract, decoder = g("exp")[...], g("con")[...], g("dec")[...]

        def chunk(c, carry):
            lanes = pl.ds(pl.multiple_of(c * 256, 256), 256)
            own = pl.ds(pl.multiple_of(c * 256 + w, 128), 256)
            x = g("mix")[:, lanes]
            x = x - jnp.mean(x, axis=0, keepdims=True)
            rstd = lax.rsqrt(jnp.mean(x * x, axis=0, keepdims=True) + 1e-06)
            x = x * rstd
            g("nrm")[step, :, lanes] = x
            g("rstd")[step, :, lanes] = rstd
            v = nn(expand, x.astype(BF))
            u = v * v
            t = jnp.tanh(v * (C0 + (C0 * C1) * u))
            half = 0.5 + 0.5 * t
            g("dgelu")[step, :, lanes] = half + (0.5 * v) * (1.0 - t * t) * (C0 + (3.0 * C0 * C1) * u)
            hid = (v * half).astype(BF)
            g("hid")[step, :, lanes] = hid
            res = (fp[step, :, own] + nn(contract, hid)).astype(BF)
            g("resb")[step, :, lanes] = res
            g("out")[:, lanes] = nn(decoder, res)
            return carry

        lax.fori_loop(0, SL // 256, chunk, 0)

    def backward(m, step):
        g = weights(m)
        w, rows = m.width, m.rows
        decoder_t, contract_t, expand_t = g("dect")[...], g("cont")[...], g("expt")[...]

        def chunk(c, carry):
            lanes = pl.ds(pl.multiple_of(c * 256, 256), 256)
            dy = g("cot")[:, lanes]
            if m is SEA:
                dy = dy * r.wetf[:, lanes]
            dy = dy.astype(BF)
            g("dyb")[:, lanes] = dy
            dres = nn(decoder_t, dy).astype(BF)
            g("dresb")[:, lanes] = dres
            dhid = nn(contract_t, dres)
            dpre = (dhid * g("dgelu")[step, :, lanes]).astype(BF)
            g("dpreb")[:, lanes] = dpre
            dn = nn(expand_t, dpre)
            x = g("nrm")[step, :, lanes]
            dmean = jnp.mean(dn, axis=0, keepdims=True)
            dproj = jnp.mean(dn * x, axis=0, keepdims=True)
            g("dmr")[1, :, lanes] = g("rstd")[step, :, lanes] * (dn - dmean - x * dproj)
            return carry

        lax.fori_loop(0, SL // 256, chunk, 0)
        fp, dmr = g("fp"), g("dmr")
        dw = g("dw")[...]
        for row in range(rows):
            lanes = slice(row * w, (row + 1) * w)
            d = dmr[1, :, lanes]
            dmr[0, :, lanes] = roll(d, -1)
            dmr[2, :, lanes] = roll(d, 1)
        spare = None
        for q in range(rows + 1, -1, -1):
            total = None
            for i in range(3):
                row = q - i
                if 0 <= row < rows:
                    for j in range(3):
                        term = dw[:, 3 * i + j : 3 * i + j + 1] * dmr[j, :, row * w : (row + 1) * w]
                        total = term if total is None else total + term
            if 1 <= q <= rows:
                total = total + g("dresb")[:, (q - 1) * w : q * w].astype(F32)
            if q == rows + 1:
                if m is SEA:
                    spare = last_f * nt(total.astype(BF), r.fold[...])
                total = total * up_on
            if q == rows and m is SEA:
                total = total + spare
            if q == 0:
                total = total * low_on
            total = total.astype(BF)
            for i in range(3):
                g("dfs")[i * 64 : (i + 1) * 64, (q + i) * w : (q + i + 1) * w] = total
        enc_t = g("enct")[...]
        kc = m.chans
        for row in range(rows + 4):
            lanes = slice(row * w, (row + 1) * w)
            d = nn(enc_t, g("dfs")[:, lanes])
            g("dx")[:, lanes] = d[kc : 2 * kc] + roll(d[0:kc], -1) + roll(d[2 * kc : 3 * kc], 1)

    def weight_grads(m, step):
        g = weights(m)
        w, rows = m.width, m.rows
        row0 = 0 if m is SEA else 64
        fp, dmr = g("fp"), g("dmr")
        exp = nt(g("nrm")[step].astype(BF), g("dpreb")[...])
        for half in range(2):
            start = G_EXP + 2 * row0 + half * 64
            r.g32[start : start + 64, :] += exp[:, half * 128 : (half + 1) * 128]
        con = nt(g("dresb")[...], g("hid")[step])
        for half in range(2):
            start = G_CON + 2 * row0 + half * 64
            r.g32[start : start + 64, :] += con[:, half * 128 : (half + 1) * 128]
        dec = nt(g("dyb")[...], g("resb")[step])
        start = G_DEC + (0 if m is SEA else 48)
        r.g32[start : start + m.outs, 0:64] += dec
        enc = nt(g("dfs")[...], g("s3")[step])
        if m is SEA:
            r.g32[G_ENC0 : G_ENC0 + 192, :] += enc[:, 0:128]
            r.g32[G_ENC1 : G_ENC1 + 192, 0:64] += enc[:, 128:192]
        else:
            r.g32[G_ENC1 : G_ENC1 + 192, 64 : 64 + 48] += enc
        for i in range(3):
            for j in range(3):
                total = None
                for row in range(rows):
                    term = dmr[j, :, row * w : (row + 1) * w] * fp[step, :, (row + i) * w : (row + i + 1) * w]
                    total = term if total is None else total + term
                t = 3 * i + j + (0 if m is SEA else 16)
                r.g32[G_DW : G_DW + 64, t : t + 1] += jnp.sum(total, axis=1, keepdims=True)

    def regrid_flux(step, sent):
        wait(sent)
        flow = regrid(
            field_of(r.pay_f, r.in_f, step, False), True,
            r.oh_sa, s_air, r.oh_ss, s_sea, lambda k: own_weight(k, 2),
        )
        r.pay_g[step] = flow
        sent = [
            send(r.pay_g.at[step], r.in_g.at[step, i], near(off)) for i, off in enumerate((-1, 1))
        ]
        for hi in range(8):
            r.sea_x[48:52, SL + hi * 128 : SL + (hi + 1) * 128] = r.pay_g[step, hi * 4 : hi * 4 + 4, :]
        return sent

    def regrid_surface(step, sent):
        wait(sent)
        skin = regrid(
            field_of(r.pay_s, r.in_s, step, True), False,
            r.oh_as, a_sea, r.oh_aa, a_air, lambda k: air_meta(k, 1),
        )
        r.pay_k[step] = skin
        sent = [
            send(r.pay_k.at[step], r.in_k.at[step, i], near(off)) for i, off in enumerate((-1, 1))
        ]
        for hi in range(8):
            r.air_x[8:9, 256 + hi * 128 : 256 + (hi + 1) * 128] = r.pay_k[step, hi : hi + 1, :]
        return sent

    def sea_states(step, sent):
        wait(sent)
        own = r.halo_s[1] if step else r.halo_s_in[0, 1]
        r.sea_x[0:48, SL : 2 * SL] = own.astype(F32)
        if step == 0:
            r.o_now[...] = own.astype(F32)
        r.sea_x[0:48, 0:SL] = r.halo_s_in[step, 2].astype(F32) * low_on
        r.sea_x[0:48, 2 * SL : 3 * SL] = r.halo_s_in[step, 0].astype(F32) * up_on
        folded = nn(own[:, 512:SL], r.fold[...])
        r.sea_x[0:48, 2 * SL : 2 * SL + 512] += last_f * folded
        stack_taps(SEA, step, range(6), (0, 48))

    def sea_forward(step, sent):
        wait(sent)
        for hi in range(8):
            r.sea_x[48:52, hi * 128 : (hi + 1) * 128] = r.in_g[step, 1, hi * 4 : hi * 4 + 4, :] * low_on
            r.sea_x[48:52, 2 * SL + hi * 128 : 2 * SL + (hi + 1) * 128] = (
                r.in_g[step, 0, hi * 4 : hi * 4 + 4, :] * up_on
            )
        folded = nn(r.sea_x[48:64, SL + 512 : 2 * SL].astype(BF), r.fold[...])
        r.sea_x[48:64, 2 * SL : 2 * SL + 512] += last_f * folded
        stack_taps(SEA, step, range(6), (48, 64))
        forward(SEA, step)
        r.o_now[...] += r.wetf[...] * r.sea_out[...]

    def air_states(step, sent):
        wait(sent)
        if step == 0:
            r.a_now[...] = r.band_a_in[...]
        r.air_x[0:8, 256 : 256 + SL] = r.a_now[...]
        r.air_x[0:8, 0:256] = r.halo_a_in[step, 1] * low_on
        r.air_x[0:8, 256 + SL : 512 + SL] = r.halo_a_in[step, 0] * up_on

    def air_forward(step, sent):
        wait(sent)
        for i in range(2):
            r.air_x[8:9, i * 128 : (i + 1) * 128] = r.in_k[step, 1, 6 + i : 7 + i, :] * low_on
            r.air_x[8:9, 256 + SL + i * 128 : 256 + SL + (i + 1) * 128] = (
                r.in_k[step, 0, i : i + 1, :] * up_on
            )
        stack_taps(AIR, step, range(12), (0, 16))
        forward(AIR, step)
        r.a_now[...] += r.air_out[0:8, :]

    def start_c_sea(step):
        copies = []
        for i, off in enumerate((-1, 1)):
            lanes = slice(i * 2 * SL, i * 2 * SL + SL)
            r.ret_g[step, i] = r.sea_dx[48:56, lanes]
            copies.append(send(r.ret_g.at[step, i], r.ret_g_in.at[step, i], near(off)))
        for i, off in enumerate((-1, 1)):
            lanes = slice(i * 2 * SL, i * 2 * SL + SL)
            r.ret_s[step, i] = r.sea_dx[0:48, lanes].astype(BF)
            copies.append(send(r.ret_s.at[step, i], r.ret_s_in.at[step, i], near(off)))
        back = nt(r.sea_dx[:, 2 * SL : 2 * SL + 512].astype(BF), r.fold[...])
        r.sea_dx[:, SL + 512 : 2 * SL] += last_f * back
        return copies

    def start_c_air(step):
        copies = []
        for i, off in enumerate((-1, 1)):
            start = i * (256 + SL)
            r.ret_a[step, i] = r.air_dx[:, start : start + 256]
            copies.append(send(r.ret_a.at[step, i], r.ret_a_in.at[step, i], near(off)))
        return copies

    def start_dg(step, sent):
        wait(sent[0:2])
        own = slice(SL, 2 * SL)
        r.sea_dx[48:56, own] += r.ret_g_in[step, 1] * low_on + r.ret_g_in[step, 0] * up_on
        for hi in range(8):
            r.pay_dg[step, hi * 4 : hi * 4 + 4, :] = r.sea_dx[48:52, SL + hi * 128 : SL + (hi + 1) * 128]
        return [send(r.pay_dg.at[step], r.in_dg.at[step, i], near(off)) for i, off in enumerate(OFFS)]

    def start_dk(step, sent):
        wait(sent)
        own = slice(256, 512)
        r.air_dx[:, own] += r.ret_a_in[step, 1] * low_on
        own = slice(SL, SL + 256)
        r.air_dx[:, own] += r.ret_a_in[step, 0] * up_on
        for hi in range(8):
            r.pay_dk[step, hi : hi + 1, :] = r.air_dx[8:9, 256 + hi * 128 : 256 + (hi + 1) * 128]
        sent = [send(r.pay_dk.at[step], r.in_dk.at[step, i], near(off)) for i, off in enumerate(OFFS)]
        r.air_cot[0:8, :] += r.air_dx[0:8, 256 : 256 + SL]
        return sent

    def finish_sea_cot(step, sent):
        wait(sent[2:4])
        r.sea_cot[...] += (
            r.sea_dx[0:48, SL : 2 * SL]
            + r.ret_s_in[step, 1].astype(F32) * low_on
            + r.ret_s_in[step, 0].astype(F32) * up_on
        )

    def finish_dg(step, sent):
        wait(sent)
        r.tmp32[...] = regrid(
            field_of(r.pay_dg, r.in_dg, step, True), True,
            r.oh_as, a_sea, r.oh_aa, a_air, lambda k: air_meta(k, 2),
        )
        for hi in range(8):
            r.air_cot[8:12, hi * 128 : (hi + 1) * 128] = r.tmp32[hi * 4 : hi * 4 + 4, :]

    def finish_dk(step, sent):
        wait(sent)
        r.tmp8[...] = regrid(
            field_of(r.pay_dk, r.in_dk, step, False), False,
            r.oh_sa, s_air, r.oh_ss, s_sea, lambda k: own_weight(k, 1),
        )
        for hi in range(8):
            r.sea_cot[0:1, hi * 128 : (hi + 1) * 128] += r.tmp8[hi : hi + 1, :]

    wait(own_sea)
    halo_sea = [
        send(r.halo_s_in.at[0, 1], r.halo_s_in.at[0, off + 1], near(off)) for off in (-1, 1)
    ]
    sent_k = regrid_surface(0, sent_s)
    sent_g = regrid_flux(0, sent_f)
    sent_cot = [give(r.cota, r.cota_in, served(0)), give(r.cots, r.cots_in, served(0))]
    air_states(0, halo_air)
    sea_states(0, halo_sea)
    air_forward(0, sent_k)
    for hi in range(8):
        r.new_f[hi * 4 : hi * 4 + 4, :] = r.air_out[8:12, hi * 128 : (hi + 1) * 128]
    r.pay_f[1] = r.new_f[...].astype(BF)
    sent_f = start_f(1)
    halo_air = start_halo_air(1)
    sea_forward(0, sent_g)
    sent_s = start_s(1)
    halo_sea = start_halo_sea(1)

    air_states(1, halo_air)
    sent_g = regrid_flux(1, sent_f)
    sea_states(1, halo_sea)
    sent_k = regrid_surface(1, sent_s)
    sea_forward(1, sent_g)
    wait(sent_cot)
    r.sea_cot[...] = r.cots_in[...].astype(F32)
    r.air_cot[0:8, :] = r.cota_in[...]
    r.air_cot[8:16, :] = jnp.zeros((8, SL), F32)
    backward(SEA, 1)
    sea_c = start_c_sea(1)
    air_forward(1, sent_k)
    backward(AIR, 1)
    air_c = start_c_air(1)

    weight_grads(SEA, 1)
    sent_dg = start_dg(1, sea_c)
    weight_grads(AIR, 1)
    finish_sea_cot(1, sea_c)
    sent_dk = start_dk(1, air_c)
    r.back_sea[...] = r.o_now[...].astype(BF)
    home = [give(r.a_now, r.home_air, band), give(r.back_sea, r.home_sea, band)]
    finish_dg(1, sent_dg)
    backward(AIR, 0)
    air_c = start_c_air(0)
    weight_grads(AIR, 0)
    finish_dk(1, sent_dk)
    backward(SEA, 0)
    sea_c = start_c_sea(0)
    weight_grads(SEA, 0)

    for c in range(2):
        for y in range(4):
            for e in range(8):
                start = ((c * 4 + y) * 8 + e) * 16
                r.gb[c, y, e] = r.g32[start : start + 16, :].astype(BF)
    sum_core = [send(r.gb.at[1 - core], r.r1, peer_core)]
    sent_dk = start_dk(0, air_c)
    wait(sum_core)
    r.h1[...] = (r.gb[core].astype(F32) + r.r1[...].astype(F32)).astype(BF)
    sum_y = [
        send(r.h1.at[lax.rem(yy + s, 4)], r.r2.at[s - 1], peers_y[s - 1]) for s in (1, 2, 3)
    ]
    wait(home)
    for row in range(8):
        r.o_air[:, row, :] = r.home_air[:, row * 128 : (row + 1) * 128]
    for row in range(2):
        r.o_sea[:, row, :] = r.home_sea[:, row * 512 : (row + 1) * 512].astype(F32)
    sent_dg = start_dg(0, sea_c)
    wait(sum_y)
    h2 = r.h1[yy].astype(F32)
    for s in range(3):
        h2 = h2 + r.r2[s].astype(F32)
    h2 = h2.astype(BF)
    r.h2[...] = h2
    r.r3[xx] = h2
    sum_x = [send(r.h2, r.r3.at[xx], dev) for dev in peers_x]
    finish_sea_cot(0, sea_c)
    finish_dk(0, sent_dk)
    r.back_dsea[...] = r.sea_cot[...].astype(BF)
    wait(sum_x)
    h3 = r.r3[0].astype(F32)
    for s in range(1, nx):
        h3 = h3 + r.r3[s].astype(F32)
    h3 = h3.astype(BF)
    r.h3[...] = h3
    r.r4[zz] = h3
    sum_z = [send(r.h3, r.r4.at[zz], dev) for dev in peers_z]
    finish_dg(0, sent_dg)
    home = [give(r.air_cot, r.home_dair, band), give(r.back_dsea, r.home_dsea, band)]
    wait(sum_z)
    h4 = r.r4[0].astype(F32)
    for s in range(1, nz):
        h4 = h4 + r.r4[s].astype(F32)
    r.gout[core, yy] = h4.astype(BF)
    give_y = [send(r.gout.at[core, yy], r.gout.at[core, yy], dev) for dev in peers_y]
    wait(home)
    for row in range(8):
        lanes = slice(row * 128, (row + 1) * 128)
        r.o_dair[:, row, :] = r.home_dair[0:8, lanes]
        r.o_dflux[:, row, :] = r.home_dair[8:12, lanes]
    for row in range(2):
        r.o_dsea[:, row, :] = r.home_dsea[:, row * 512 : (row + 1) * 512].astype(F32)
    wait(give_y)
    give_core = [send(r.gout.at[core], r.gout.at[core], peer_core)]
    wait(give_core)
    r.o_grads[...] = r.gout[...]


def finish(n, *refs):
    given, results = refs[0:5], refs[6:11]
    r = Names(
        ("grads",) + tuple("o_" + m + "_" + w for m in ("air", "sea") for w in WEIGHTS) + ("g32",),
        (refs[5],) + refs[11:],
    )
    for a, b in zip(given, results):
        b[...] = a[...]
    for c in range(2):
        for y in range(4):
            for e in range(8):
                start = ((c * 4 + y) * 8 + e) * 16
                r.g32[start : start + 16, :] = r.grads[c, y, e].astype(F32)

    scale = 1.0 / math.sqrt(SL * n)
    for m in (AIR, SEA):
        o = lambda s: getattr(r, "o_" + m.name + "_" + s)
        col = 0 if m is SEA else 64
        for half in range(2):
            start = G_EXP + 2 * col + half * 64
            o("exp")[:, half * 128 : (half + 1) * 128] = r.g32[start : start + 64, :] * scale
            start = G_CON + 2 * col + half * 64
            o("con")[:, half * 128 : (half + 1) * 128] = r.g32[start : start + 64, :] * scale
        start = G_DEC + (0 if m is SEA else 48)
        count_out = 48 if m is SEA else 12
        o("dec")[...] = r.g32[start : start + count_out, 0:64] * scale
        shift = 0 if m is SEA else 16
        o("dw")[...] = (jnp.transpose(r.g32[G_DW : G_DW + 64, :]) * scale)[shift : shift + 9, :]
        chans = 52 if m is SEA else 9
        for i in range(3):
            for j in range(3):
                t = 3 * i + j
                if m is AIR:
                    base, left = G_ENC1, 64 + 16 * j
                else:
                    base, left = (G_ENC0, 64 * j) if j < 2 else (G_ENC1, 0)
                piece = r.g32[base + i * 64 : base + (i + 1) * 64, left : left + chans]
                o("enc")[:, t * chans : (t + 1) * chans] = piece * scale


def body(n, *args):
    (
        air_state, sea_state, flux, air_cells, sea_cells, counts, sea_share, air_share, partner, wet,
        air_c, sea_c, air_enc, air_dw, air_exp, air_con, air_dec, sea_enc, sea_dw, sea_exp, sea_con,
        sea_dec,
    ) = args
    slots = lambda x: jnp.transpose(x, (1, 0, 2))
    given = [
        air_state, sea_state, flux, slots(air_cells), slots(sea_cells), counts, slots(sea_share),
        slots(air_share), partner[None], wet, air_c, sea_c,
        air_enc, air_dw.T, air_exp.T, air_con, air_dec, sea_enc, sea_dw.T, sea_exp.T, sea_con, sea_dec,
    ]
    vmem = pl.BlockSpec(memory_space=pltpu.VMEM)
    fields = [jax.ShapeDtypeStruct(x.shape, F32) for x in (air_state, sea_state, air_c, sea_c, flux)]
    made = pl.pallas_call(
        lambda *refs: kernel(n, *refs),
        out_shape=fields + [jax.ShapeDtypeStruct((2, 4, 8, 16, 128), BF)],
        in_specs=[vmem] * len(given),
        out_specs=[vmem] * 6,
        scratch_shapes=[pltpu.VMEM(shape, kind) for _, shape, kind in scratch_list()]
        + [pltpu.SemaphoreType.DMA((COPIES,)), pltpu.SemaphoreType.DMA((COPIES,))],
        compiler_params=pltpu.CompilerParams(
            collective_id=0, has_side_effects=True, vmem_limit_bytes=60 * 1024 * 1024
        ),
        name="coupled",
    )(*given)
    grads = [air_enc, air_dw.T, air_exp.T, air_con, air_dec, sea_enc, sea_dw.T, sea_exp.T, sea_con, sea_dec]
    done = pl.pallas_call(
        lambda *refs: finish(n, *refs),
        out_shape=fields + [jax.ShapeDtypeStruct(x.shape, F32) for x in grads],
        in_specs=[vmem] * 6,
        out_specs=[vmem] * 15,
        scratch_shapes=[pltpu.VMEM((GROWS, 128), F32)],
        name="finish",
    )(*made)
    done = list(done)
    for i in (6, 7, 11, 12):
        done[i] = done[i].T
    return done


def solution(mesh):
    n = mesh.shape["tile"]
    rows = P(None, "tile", None)
    slots = P("tile", None, None)
    return jax.shard_map(
        lambda *args: tuple(body(n, *args)),
        mesh=mesh,
        in_specs=(rows, rows, rows, slots, slots, P("tile", None), slots, slots, P(), P("tile", None), rows, rows)
        + (P(),) * 10,
        out_specs=(rows,) * 5 + (P(),) * 10,
        check_vma=False,
    )
```

```python
import math

import jax
import jax.numpy as jnp
from jax import lax
from jax.experimental import pallas as pl
from jax.experimental.pallas import tpu as pltpu
from jax.sharding import PartitionSpec as P

MESH = pl.DeviceIdType.MESH
F32 = jnp.float32
BF = jnp.bfloat16
OFFS = (-2, -1, 1, 2)
AROUND = (-2, -1, 0, 1, 2)
NEAR = 5
SL = 1024
PART = 1024
C0 = math.sqrt(2.0 / math.pi)
C1 = 0.044715


def nn(a, b):
    return jnp.dot(a, b, preferred_element_type=F32)


def nt(a, b):
    return lax.dot_general(a, b, (((1,), (1,)), ((), ())), preferred_element_type=F32)


def tn(a, b):
    return lax.dot_general(a, b, (((0,), (0,)), ((), ())), preferred_element_type=F32)


def roll(x, by):
    return pltpu.roll(x, by % x.shape[1], axis=1)


def at_band(z, xr, y, core, nx, flip):
    return ((z * nx + xr) * 4 + flip(y, 4, lax.rem(xr, 2))) * 2 + core


class Either:
    def __init__(self, own, local, remote):
        self.own, self.local, self.remote = own, local, remote

    def start(self):
        pl.when(self.own)(self.local.start)
        pl.when(jnp.logical_not(self.own))(self.remote.start)

    def wait(self):
        pl.when(self.own)(self.local.wait)
        pl.when(jnp.logical_not(self.own))(self.remote.wait)


class Names:
    def __init__(self, names, refs):
        for name, ref in zip(names, refs):
            setattr(self, name, ref)


class Model:
    def __init__(self, name, rows, width, state, inputs, chans, given, outs):
        self.name, self.rows, self.width = name, rows, width
        self.state, self.chans, self.outs = state, chans, outs
        self.inputs, self.given = inputs, given
        self.ext = (rows + 4) * width
        self.pad = (rows + 2) * width

    def scratch(self):
        f, b = F32, BF
        n, kc = self.name, self.chans
        return [
            (n + "_x", (kc, self.ext), f),
            (n + "_s3", (2, 3 * kc, self.ext), b),
            (n + "_y", (192, self.ext), f),
            (n + "_fp", (2, 64, self.pad), f),
            (n + "_mix", (64, SL), f),
            (n + "_nrm", (2, 64, SL), f),
            (n + "_rstd", (2, 1, SL), f),
            (n + "_dgelu", (2, 256, SL), f),
            (n + "_hid", (2, 256, SL), b),
            (n + "_resb", (2, 64, SL), b),
            (n + "_out", (self.outs, SL), f),
            (n + "_cot", (self.outs, SL), f),
            (n + "_dyb", (self.outs, SL), b),
            (n + "_dresb", (64, SL), b),
            (n + "_dpreb", (256, SL), b),
            (n + "_dmr", (3, 64, SL), f),
            (n + "_dfs", (192, self.ext), b),
            (n + "_ds3", (3 * kc, self.ext), f),
            (n + "_dx", (kc, self.ext), f),
            (n + "_encf", (192, 3 * kc), f),
            (n + "_enc", (192, 3 * kc), b),
            (n + "_enct", (3 * kc, 192), b),
            (n + "_exp", (256, 64), b),
            (n + "_cont", (256, 64), b),
            (n + "_decf", (self.outs, 64), f),
            (n + "_dec", (self.outs, 64), b),
            (n + "_dect", (64, self.outs), b),
            (n + "_dw", (64, 16), f),
        ]


AIR = Model("air", 8, 128, 8, 9, 16, 12, 16)
SEA = Model("sea", 2, 512, 48, 52, 64, 48, 48)

INPUTS = (
    "air_state",
    "sea_state",
    "flux",
    "air_cells",
    "sea_cells",
    "counts",
    "sea_share",
    "air_share",
    "partner",
    "wet",
    "air_c",
    "sea_c",
    "air_renc",
    "air_rdw",
    "air_expt",
    "air_con",
    "air_rdec",
    "sea_renc",
    "sea_rdw",
    "sea_expt",
    "sea_con",
    "sea_rdec",
)
OUTPUTS = ("o_air", "o_sea", "o_dair", "o_dsea", "o_dflux", "o_grads")
WEIGHTS = ("enc", "dw", "exp", "con", "dec")

COPIES = 96
GROWS = 1024
G_EXP, G_CON, G_ENC0, G_ENC1, G_DEC, G_DW = 0, 256, 512, 704, 896, 960


def scratch_list():
    f, b = F32, BF
    items = AIR.scratch() + SEA.scratch()
    items += [
        ("meta_pay", (4, 4, SL), f),
        ("meta_in", (4, 4, SL), f),
        ("own_f", (32, SL), f),
        ("own_pay", (32, SL), b),
        ("own_in", (32, SL), b),
        ("own", (24, SL), f),
        ("band_a", (8, SL), f),
        ("band_a_in", (8, SL), f),
        ("cots", (48, SL), b),
        ("cots_in", (48, SL), b),
        ("cota", (8, SL), f),
        ("cota_in", (8, SL), f),
        ("home_air", (8, SL), f),
        ("home_sea", (48, SL), b),
        ("back_sea", (48, SL), b),
        ("home_dair", (16, SL), f),
        ("home_dsea", (48, SL), b),
        ("back_dsea", (48, SL), b),
        ("oh_aa", (128, NEAR * SL), b),
        ("oh_as", (128, NEAR * SL), b),
        ("oh_sa", (128, NEAR * SL), b),
        ("oh_ss", (128, NEAR * SL), b),
        ("fold", (512, 512), b),
        ("wetf", (1, SL), f),
        ("a_now", (8, SL), f),
        ("o_now", (48, SL), f),
        ("new_f", (32, 128), f),
        ("pay_f", (2, 32, 128), b),
        ("in_f", (2, 5, 32, 128), b),
        ("pay_s", (2, 8, 128), f),
        ("in_s", (2, 5, 8, 128), f),
        ("halo_s", (2, 48, SL), b),
        ("halo_s_in", (2, 3, 48, SL), b),
        ("halo_a", (2, 2, 8, 256), f),
        ("halo_a_in", (2, 2, 8, 256), f),
        ("pay_g", (2, 32, 128), f),
        ("in_g", (2, 2, 32, 128), f),
        ("pay_k", (2, 8, 128), f),
        ("in_k", (2, 2, 8, 128), f),
        ("ret_s", (2, 2, 48, SL), b),
        ("ret_s_in", (2, 2, 48, SL), b),
        ("ret_g", (2, 2, 8, SL), f),
        ("ret_g_in", (2, 2, 8, SL), f),
        ("ret_a", (2, 2, 16, 256), f),
        ("ret_a_in", (2, 2, 16, 256), f),
        ("pay_dg", (2, 32, 128), f),
        ("in_dg", (2, 4, 32, 128), f),
        ("pay_dk", (2, 8, 128), f),
        ("in_dk", (2, 4, 8, 128), f),
        ("tmp32", (32, 128), f),
        ("tmp8", (8, 128), f),
        ("g32", (GROWS, 128), f),
        ("gb", (2, 4, 8, 16, 128), b),
        ("r1", (4, 8, 16, 128), b),
        ("h1", (4, 8, 16, 128), b),
        ("r2", (3, 8, 16, 128), b),
        ("h2", (8, 16, 128), b),
        ("r3", (4, 8, 16, 128), b),
        ("h3", (8, 16, 128), b),
        ("r4", (4, 8, 16, 128), b),
        ("gout", (2, 4, 8, 16, 128), b),
    ]
    return items


def kernel(n, *refs):
    names = INPUTS + OUTPUTS + tuple(item[0] for item in scratch_list()) + ("ssem", "rsem")
    r = Names(names, refs)
    me = lax.axis_index("tile")
    core = lax.rem(me, 2)
    yy = lax.rem(me // 2, 4)
    nx = min(4, n // 8)
    nz = n // (8 * nx)
    xx = lax.rem(me // 8, nx)
    zz = me // (8 * nx)

    def flip(value, size, odd):
        return value + odd * (size - 1 - 2 * value)

    def worker(band):
        c, chip = lax.rem(band, 2), band // 2
        z, xr, yr = chip // (4 * nx), lax.rem(chip // 4, nx), lax.rem(chip, 4)
        x = flip(xr, nx, lax.rem(z, 2))
        y = flip(yr, 4, lax.rem(xr, 2))
        return ((z * nx + x) * 4 + y) * 2 + c

    band = at_band(zz, flip(xx, nx, lax.rem(zz, 2)), yy, core, nx, flip)
    first = band == 0
    last = band == n - 1
    low_on = jnp.where(first, 0.0, 1.0).astype(F32)
    up_on = jnp.where(last, 0.0, 1.0).astype(F32)
    last_f = 1.0 - up_on

    def near(off):
        return worker(lax.rem(band + (off + n), n))

    def served(off):
        return worker(lax.rem(me + (off + n), n))

    def at(z, x, y, c):
        return ((z * nx + x) * 4 + y) * 2 + c

    peer_core = at(zz, xx, yy, 1 - core)
    peers_y = [at(zz, xx, lax.rem(yy + s, 4), core) for s in (1, 2, 3)]
    peers_x = [at(zz, lax.rem(xx + s, nx), yy, core) for s in range(1, nx)]
    peers_z = [at(lax.rem(zz + s, nz), xx, yy, core) for s in range(1, nz)]

    count = [0]

    def give(src, dst, dev):
        i = count[0]
        count[0] += 1
        remote = pltpu.make_async_remote_copy(
            src_ref=src,
            dst_ref=dst,
            send_sem=r.ssem.at[i],
            recv_sem=r.rsem.at[i],
            device_id=(dev,),
            device_id_type=MESH,
        )
        copy = Either(dev == me, pltpu.make_async_copy(src, dst, r.rsem.at[i]), remote)
        copy.start()
        return copy

    def send(src, dst, dev):
        i = count[0]
        count[0] += 1
        copy = pltpu.make_async_remote_copy(
            src_ref=src,
            dst_ref=dst,
            send_sem=r.ssem.at[i],
            recv_sem=r.rsem.at[i],
            device_id=(dev,),
            device_id_type=MESH,
        )
        copy.start()
        return copy

    def wait(copies):
        for copy in copies:
            copy.wait()

    iota8 = lax.broadcasted_iota(jnp.int32, (8, SL), 0)
    iota32 = lax.broadcasted_iota(jnp.int32, (32, SL), 0) // 4

    senders = [near(off) for off in OFFS] + peers_y + peers_x + peers_z
    barrier = pltpu.get_barrier_semaphore()
    for dev in senders:
        pl.semaphore_signal(barrier, inc=1, device_id=(dev,), device_id_type=MESH)
    either = [lax.rem(band + (n - off), n) for off in AROUND] + [worker(me)]

    def greet(dev):
        def there():
            pl.semaphore_signal(barrier, inc=1, device_id=(dev,), device_id_type=MESH)

        pl.when(dev != me)(there)

    greetings = len(senders)
    for dev in either:
        greet(dev)
        greetings = greetings + (dev != me).astype(jnp.int32)

    lane = lax.broadcasted_iota(jnp.int32, (1, SL), 1)

    def slot_rows(k_out, k_air, put):
        used = lane < r.counts[0:1, k_out : k_out + 1]
        put(0, r.sea_cells[k_out].astype(F32))
        put(1, jnp.where(used, r.air_share[k_out], 0.0))
        put(2, jnp.where(used, r.sea_share[k_out], 0.0))
        put(3, r.air_cells[k_air].astype(F32))

    for i, off in enumerate(OFFS):

        def put(row, value, i=i):
            r.meta_pay[i, row : row + 1, :] = value

        slot_rows(off + 2, 2 - off, put)
    for k in range(NEAR):

        def put(row, value, k=k):
            base = 6 * k
            if row in (1, 2):
                r.own_f[base + 3 + row : base + 4 + row, :] = value
            else:
                high = jnp.floor(value * (1.0 / 128.0))
                start = base + (0 if row == 0 else 2)
                r.own_f[start : start + 1, :] = high
                r.own_f[start + 1 : start + 2, :] = value - 128.0 * high

        slot_rows(k, k, put)
    r.own_f[31:32, :] = jnp.zeros((1, SL), F32)
    for row in range(8):
        lanes = slice(row * 128, (row + 1) * 128)
        r.band_a[:, lanes] = r.air_state[:, row, :]
        r.cota[:, lanes] = r.air_c[:, row, :]
        r.new_f[row * 4 : row * 4 + 4, :] = r.flux[:, row, :]
    for row in range(2):
        lanes = slice(row * 512, (row + 1) * 512)
        r.halo_s[0, :, lanes] = r.sea_state[:, row, :].astype(BF)
        r.own_f[30:31, lanes] = r.wet[row : row + 1, :].astype(F32)
    for hi in range(8):
        row, left = hi // 4, (hi % 4) * 128
        r.pay_s[0, hi : hi + 1, :] = r.sea_state[0, row : row + 1, left : left + 128]
    r.pay_f[0] = r.new_f[...].astype(BF)
    r.own_pay[...] = r.own_f[...].astype(BF)
    r.halo_a[0, 0] = r.band_a[:, 0:256]
    r.halo_a[0, 1] = r.band_a[:, SL - 256 : SL]

    def start_f(step):
        return [send(r.pay_f.at[step], r.in_f.at[step, off + 2], near(off)) for off in OFFS]

    def start_s(step):
        for hi in range(8):
            r.pay_s[step, hi : hi + 1, :] = r.o_now[0:1, hi * 128 : (hi + 1) * 128]
        return [send(r.pay_s.at[step], r.in_s.at[step, off + 2], near(off)) for off in OFFS]

    def start_halo_sea(step):
        r.halo_s[step] = r.o_now[...].astype(BF)
        return [
            send(r.halo_s.at[step], r.halo_s_in.at[step, off + 1], near(off))
            for off in (-1, 1)
        ]

    def start_halo_air(step):
        r.halo_a[step, 0] = r.a_now[:, 0:256]
        r.halo_a[step, 1] = r.a_now[:, SL - 256 : SL]
        return [
            send(r.halo_a.at[step, i], r.halo_a_in.at[step, i], near(off))
            for i, off in enumerate((-1, 1))
        ]

    pl.semaphore_wait(barrier, greetings)
    metas = [give(r.own_pay, r.own_in, served(0))]
    for i, off in enumerate(OFFS):
        metas.append(give(r.meta_pay.at[i], r.meta_in.at[i], served(off)))
    sent_s = [give(r.pay_s.at[0], r.in_s.at[0, off + 2], served(off)) for off in AROUND]
    sent_f = [give(r.pay_f.at[0], r.in_f.at[0, off + 2], served(off)) for off in AROUND]
    halo_air = [give(r.band_a, r.band_a_in, served(0))]
    for i, off in enumerate((-1, 1)):
        halo_air.append(give(r.halo_a.at[0, i], r.halo_a_in.at[0, i], served(off)))
    own_sea = [give(r.halo_s.at[0], r.halo_s_in.at[0, 1], served(0))]
    for row in range(2):
        lanes = slice(row * 512, (row + 1) * 512)
        r.cots[:, lanes] = r.sea_c[:, row, :].astype(BF)

    r.g32[...] = jnp.zeros_like(r.g32)
    for m in (AIR, SEA):
        x = getattr(r, m.name + "_x")
        x[m.state : m.chans, :] = jnp.zeros((m.chans - m.state, m.ext), F32)
        dfs = getattr(r, m.name + "_dfs")
        dfs[...] = jnp.zeros_like(dfs)
        g = lambda s: getattr(r, m.name + "_" + s)
        kc, chans = m.chans, m.inputs
        g("encf")[...] = jnp.zeros_like(g("encf"))
        raw = g("renc")[...].astype(F32)
        for i in range(3):
            for j in range(3):
                t = 3 * i + j
                g("encf")[i * 64 : (i + 1) * 64, j * kc : j * kc + chans] = raw[:, t * chans : (t + 1) * chans]
        enc = g("encf")[...]
        g("enc")[...] = enc.astype(BF)
        g("enct")[...] = jnp.transpose(enc).astype(BF)
        g("exp")[...] = jnp.transpose(g("expt")[...].astype(F32)).astype(BF)
        g("cont")[...] = jnp.transpose(g("con")[...].astype(F32)).astype(BF)
        g("decf")[...] = jnp.zeros_like(g("decf"))
        g("decf")[0 : m.given, :] = g("rdec")[...].astype(F32)
        dec = g("decf")[...]
        g("dec")[...] = dec.astype(BF)
        g("dect")[...] = jnp.transpose(dec).astype(BF)
        taps = jnp.concatenate([g("rdw")[...].astype(F32), jnp.zeros((7, 64), F32)], axis=0)
        g("dw")[...] = jnp.transpose(taps)
    source = lax.broadcasted_iota(jnp.int32, (512, 512), 0)
    r.fold[...] = jnp.where(source == r.partner[...], 1.0, 0.0).astype(BF)
    iota128 = lax.broadcasted_iota(jnp.int32, (128, SL), 0)

    def one_hot(row):
        low = jnp.bitwise_and(row, 127)
        return jnp.where(iota128 == low, 1.0, 0.0).astype(BF)

    def own_row(k, row):
        return r.own[4 * k + row : 4 * k + row + 1, :]

    def air_meta(k, row):
        if k == 2:
            return own_row(2, row)
        return r.meta_in[OFFS.index(k - 2), row : row + 1, :]

    def sea_meta(k, row):
        return air_meta(4 - k, row)

    def own_weight(k, row):
        return own_row(k, row)

    def a_air(k):
        return own_row(k, 3).astype(jnp.int32)

    def a_sea(k):
        return air_meta(k, 0).astype(jnp.int32)

    def s_sea(k):
        return own_row(k, 0).astype(jnp.int32)

    def s_air(k):
        return sea_meta(k, 3).astype(jnp.int32)

    wait(metas)
    arrived = r.own_in[...].astype(F32)
    for k in range(NEAR):
        base = 6 * k
        r.own[4 * k : 4 * k + 1, :] = arrived[base : base + 1] * 128.0 + arrived[base + 1 : base + 2]
        r.own[4 * k + 1 : 4 * k + 3, :] = arrived[base + 4 : base + 6]
        r.own[4 * k + 3 : 4 * k + 4, :] = arrived[base + 2 : base + 3] * 128.0 + arrived[base + 3 : base + 4]
    r.wetf[...] = arrived[30:31]
    for k in range(NEAR):
        lanes = slice(k * SL, (k + 1) * SL)
        r.oh_aa[:, lanes] = one_hot(a_air(k))
        r.oh_ss[:, lanes] = one_hot(s_sea(k))
        r.oh_as[:, lanes] = one_hot(a_sea(k))
        r.oh_sa[:, lanes] = one_hot(s_air(k))

    def high(row):
        return jnp.right_shift(row, 7)

    def regrid(field, wide, src_oh, src_cell, dst_oh, dst_cell, weight):
        iota = iota32 if wide else iota8
        total = None
        for k in range(NEAR):
            lanes = slice(k * SL, (k + 1) * SL)
            picked = nn(field(k).astype(BF), src_oh[:, lanes])
            picked = jnp.where(iota == high(src_cell(k)), picked, 0.0)
            if wide:
                value = (picked[0:8] + picked[8:16]) + (picked[16:24] + picked[24:32])
                value = value + pltpu.roll(value, 4, axis=0)
                value = value * weight(k)
                value = jnp.concatenate([value] * 4, axis=0)
            else:
                value = jnp.sum(picked, axis=0, keepdims=True) * weight(k)
            spread = jnp.where(iota == high(dst_cell(k)), value, 0.0).astype(BF)
            part = nt(spread, dst_oh[:, lanes])
            total = part if total is None else total + part
        return total

    def field_of(own, arrived, step, by_air):
        def get(k):
            off = k - 2 if by_air else 2 - k
            if off == 0 and not (arrived.shape[1] == NEAR and step == 0):
                return own[step]
            return arrived[step, (AROUND if arrived.shape[1] == NEAR else OFFS).index(off)]

        return get

    def weights(m):
        g = lambda s: getattr(r, m.name + "_" + s)
        return g

    def stack_taps(m, step, rows, channels):
        g = weights(m)
        w, kc = m.width, m.chans
        lo, hi = channels
        for row in rows:
            lanes = slice(row * w, (row + 1) * w)
            x = g("x")[lo:hi, lanes]
            g("s3")[step, lo:hi, lanes] = roll(x, 1).astype(BF)
            g("s3")[step, kc + lo : kc + hi, lanes] = x.astype(BF)
            g("s3")[step, 2 * kc + lo : 2 * kc + hi, lanes] = roll(x, -1).astype(BF)

    def forward(m, step):
        g = weights(m)
        w, rows = m.width, m.rows
        enc = g("enc")[...]
        for row in range(rows + 4):
            lanes = slice(row * w, (row + 1) * w)
            g("y")[:, lanes] = nn(enc, g("s3")[step, :, lanes])
        fp, y = g("fp"), g("y")
        for q in list(range(rows + 2)):
            feat = y[0:64, q * w : (q + 1) * w]
            feat = feat + y[64:128, (q + 1) * w : (q + 2) * w]
            feat = feat + y[128:192, (q + 2) * w : (q + 3) * w]
            feat = feat.astype(BF).astype(F32)
            if q == 0:
                feat = feat * low_on
            if q == rows + 1:
                feat = feat * up_on
                if m is SEA:
                    below = fp[step, :, rows * w : (rows + 1) * w].astype(BF)
                    feat = feat + last_f * nn(below, r.fold[...])
            fp[step, :, q * w : (q + 1) * w] = feat
        dw = g("dw")[...]
        for row in range(rows):
            mixed = []
            for j in range(3):
                part = None
                for i in range(3):
                    term = dw[:, 3 * i + j : 3 * i + j + 1] * fp[step, :, (row + i) * w : (row + i + 1) * w]
                    part = term if part is None else part + term
                mixed.append(part)
            g("mix")[:, row * w : (row + 1) * w] = mixed[1] + roll(mixed[0], 1) + roll(mixed[2], -1)
        expand, contract, decoder = g("exp")[...], g("con")[...], g("dec")[...]

        def chunk(c):
            lanes = slice(c * PART, (c + 1) * PART)
            own = slice(c * PART + w, (c + 1) * PART + w)
            x = g("mix")[:, lanes]
            x = x - jnp.mean(x, axis=0, keepdims=True)
            rstd = lax.rsqrt(jnp.mean(x * x, axis=0, keepdims=True) + 1e-06)
            x = x * rstd
            g("nrm")[step, :, lanes] = x
            g("rstd")[step, :, lanes] = rstd
            v = nn(expand, x.astype(BF))
            u = v * v
            t = jnp.tanh(v * (C0 + (C0 * C1) * u))
            half = 0.5 + 0.5 * t
            g("dgelu")[step, :, lanes] = half + (0.5 * v) * (1.0 - t * t) * (C0 + (3.0 * C0 * C1) * u)
            hid = (v * half).astype(BF)
            g("hid")[step, :, lanes] = hid
            res = (fp[step, :, own] + nn(contract, hid)).astype(BF)
            g("resb")[step, :, lanes] = res
            g("out")[:, lanes] = nn(decoder, res)

        for c in range(SL // PART):
            chunk(c)

    def backward(m, step):
        g = weights(m)
        w, rows = m.width, m.rows
        decoder_t, contract_t, expand_t = g("dect")[...], g("cont")[...], g("expt")[...]

        def chunk(c):
            lanes = slice(c * PART, (c + 1) * PART)
            dy = g("cot")[:, lanes]
            if m is SEA:
                dy = dy * r.wetf[:, lanes]
            dy = dy.astype(BF)
            g("dyb")[:, lanes] = dy
            dres = nn(decoder_t, dy).astype(BF)
            g("dresb")[:, lanes] = dres
            dhid = nn(contract_t, dres)
            dpre = (dhid * g("dgelu")[step, :, lanes]).astype(BF)
            g("dpreb")[:, lanes] = dpre
            dn = nn(expand_t, dpre)
            x = g("nrm")[step, :, lanes]
            dmean = jnp.mean(dn, axis=0, keepdims=True)
            dproj = jnp.mean(dn * x, axis=0, keepdims=True)
            g("dmr")[1, :, lanes] = g("rstd")[step, :, lanes] * (dn - dmean - x * dproj)

        for c in range(SL // PART):
            chunk(c)
        fp, dmr = g("fp"), g("dmr")
        dw = g("dw")[...]
        for row in range(rows):
            lanes = slice(row * w, (row + 1) * w)
            d = dmr[1, :, lanes]
            dmr[0, :, lanes] = roll(d, -1)
            dmr[2, :, lanes] = roll(d, 1)
        spare = None
        for q in range(rows + 1, -1, -1):
            total = None
            for i in range(3):
                row = q - i
                if 0 <= row < rows:
                    for j in range(3):
                        term = dw[:, 3 * i + j : 3 * i + j + 1] * dmr[j, :, row * w : (row + 1) * w]
                        total = term if total is None else total + term
            if 1 <= q <= rows:
                total = total + g("dresb")[:, (q - 1) * w : q * w].astype(F32)
            if q == rows + 1:
                if m is SEA:
                    spare = last_f * nt(total.astype(BF), r.fold[...])
                total = total * up_on
            if q == rows and m is SEA:
                total = total + spare
            if q == 0:
                total = total * low_on
            total = total.astype(BF)
            for i in range(3):
                g("dfs")[i * 64 : (i + 1) * 64, (q + i) * w : (q + i + 1) * w] = total
        enc_t = g("enct")[...]
        kc = m.chans
        for row in range(rows + 4):
            lanes = slice(row * w, (row + 1) * w)
            d = nn(enc_t, g("dfs")[:, lanes])
            g("dx")[:, lanes] = d[kc : 2 * kc] + roll(d[0:kc], -1) + roll(d[2 * kc : 3 * kc], 1)

    def weight_grads(m, step):
        g = weights(m)
        w, rows = m.width, m.rows
        row0 = 0 if m is SEA else 64
        fp, dmr = g("fp"), g("dmr")
        exp = nt(g("nrm")[step].astype(BF), g("dpreb")[...])
        for half in range(2):
            start = G_EXP + 2 * row0 + half * 64
            r.g32[start : start + 64, :] += exp[:, half * 128 : (half + 1) * 128]
        con = nt(g("dresb")[...], g("hid")[step])
        for half in range(2):
            start = G_CON + 2 * row0 + half * 64
            r.g32[start : start + 64, :] += con[:, half * 128 : (half + 1) * 128]
        dec = nt(g("dyb")[...], g("resb")[step])
        start = G_DEC + (0 if m is SEA else 48)
        r.g32[start : start + m.outs, 0:64] += dec
        enc = nt(g("dfs")[...], g("s3")[step])
        if m is SEA:
            r.g32[G_ENC0 : G_ENC0 + 192, :] += enc[:, 0:128]
            r.g32[G_ENC1 : G_ENC1 + 192, 0:64] += enc[:, 128:192]
        else:
            r.g32[G_ENC1 : G_ENC1 + 192, 64 : 64 + 48] += enc
        for i in range(3):
            for j in range(3):
                total = None
                for row in range(rows):
                    term = dmr[j, :, row * w : (row + 1) * w] * fp[step, :, (row + i) * w : (row + i + 1) * w]
                    total = term if total is None else total + term
                t = 3 * i + j + (0 if m is SEA else 16)
                r.g32[G_DW : G_DW + 64, t : t + 1] += jnp.sum(total, axis=1, keepdims=True)

    def regrid_flux(step, sent):
        wait(sent)
        flow = regrid(
            field_of(r.pay_f, r.in_f, step, False), True,
            r.oh_sa, s_air, r.oh_ss, s_sea, lambda k: own_weight(k, 2),
        )
        r.pay_g[step] = flow
        sent = [
            send(r.pay_g.at[step], r.in_g.at[step, i], near(off)) for i, off in enumerate((-1, 1))
        ]
        for hi in range(8):
            r.sea_x[48:52, SL + hi * 128 : SL + (hi + 1) * 128] = r.pay_g[step, hi * 4 : hi * 4 + 4, :]
        return sent

    def regrid_surface(step, sent):
        wait(sent)
        skin = regrid(
            field_of(r.pay_s, r.in_s, step, True), False,
            r.oh_as, a_sea, r.oh_aa, a_air, lambda k: air_meta(k, 1),
        )
        r.pay_k[step] = skin
        sent = [
            send(r.pay_k.at[step], r.in_k.at[step, i], near(off)) for i, off in enumerate((-1, 1))
        ]
        for hi in range(8):
            r.air_x[8:9, 256 + hi * 128 : 256 + (hi + 1) * 128] = r.pay_k[step, hi : hi + 1, :]
        return sent

    def sea_states(step, sent):
        wait(sent)
        own = r.halo_s[1] if step else r.halo_s_in[0, 1]
        r.sea_x[0:48, SL : 2 * SL] = own.astype(F32)
        if step == 0:
            r.o_now[...] = own.astype(F32)
        r.sea_x[0:48, 0:SL] = r.halo_s_in[step, 2].astype(F32) * low_on
        r.sea_x[0:48, 2 * SL : 3 * SL] = r.halo_s_in[step, 0].astype(F32) * up_on
        folded = nn(own[:, 512:SL], r.fold[...])
        r.sea_x[0:48, 2 * SL : 2 * SL + 512] += last_f * folded
        stack_taps(SEA, step, range(6), (0, 48))

    def sea_forward(step, sent):
        wait(sent)
        for hi in range(8):
            r.sea_x[48:52, hi * 128 : (hi + 1) * 128] = r.in_g[step, 1, hi * 4 : hi * 4 + 4, :] * low_on
            r.sea_x[48:52, 2 * SL + hi * 128 : 2 * SL + (hi + 1) * 128] = (
                r.in_g[step, 0, hi * 4 : hi * 4 + 4, :] * up_on
            )
        folded = nn(r.sea_x[48:64, SL + 512 : 2 * SL].astype(BF), r.fold[...])
        r.sea_x[48:64, 2 * SL : 2 * SL + 512] += last_f * folded
        stack_taps(SEA, step, range(6), (48, 64))
        forward(SEA, step)
        r.o_now[...] += r.wetf[...] * r.sea_out[...]

    def air_states(step, sent):
        wait(sent)
        if step == 0:
            r.a_now[...] = r.band_a_in[...]
        r.air_x[0:8, 256 : 256 + SL] = r.a_now[...]
        r.air_x[0:8, 0:256] = r.halo_a_in[step, 1] * low_on
        r.air_x[0:8, 256 + SL : 512 + SL] = r.halo_a_in[step, 0] * up_on

    def air_forward(step, sent):
        wait(sent)
        for i in range(2):
            r.air_x[8:9, i * 128 : (i + 1) * 128] = r.in_k[step, 1, 6 + i : 7 + i, :] * low_on
            r.air_x[8:9, 256 + SL + i * 128 : 256 + SL + (i + 1) * 128] = (
                r.in_k[step, 0, i : i + 1, :] * up_on
            )
        stack_taps(AIR, step, range(12), (0, 16))
        forward(AIR, step)
        r.a_now[...] += r.air_out[0:8, :]

    def start_c_sea(step):
        copies = []
        for i, off in enumerate((-1, 1)):
            lanes = slice(i * 2 * SL, i * 2 * SL + SL)
            r.ret_g[step, i] = r.sea_dx[48:56, lanes]
            copies.append(send(r.ret_g.at[step, i], r.ret_g_in.at[step, i], near(off)))
        for i, off in enumerate((-1, 1)):
            lanes = slice(i * 2 * SL, i * 2 * SL + SL)
            r.ret_s[step, i] = r.sea_dx[0:48, lanes].astype(BF)
            copies.append(send(r.ret_s.at[step, i], r.ret_s_in.at[step, i], near(off)))
        back = nt(r.sea_dx[:, 2 * SL : 2 * SL + 512].astype(BF), r.fold[...])
        r.sea_dx[:, SL + 512 : 2 * SL] += last_f * back
        return copies

    def start_c_air(step):
        copies = []
        for i, off in enumerate((-1, 1)):
            start = i * (256 + SL)
            r.ret_a[step, i] = r.air_dx[:, start : start + 256]
            copies.append(send(r.ret_a.at[step, i], r.ret_a_in.at[step, i], near(off)))
        return copies

    def start_dg(step, sent):
        wait(sent[0:2])
        own = slice(SL, 2 * SL)
        r.sea_dx[48:56, own] += r.ret_g_in[step, 1] * low_on + r.ret_g_in[step, 0] * up_on
        for hi in range(8):
            r.pay_dg[step, hi * 4 : hi * 4 + 4, :] = r.sea_dx[48:52, SL + hi * 128 : SL + (hi + 1) * 128]
        return [send(r.pay_dg.at[step], r.in_dg.at[step, i], near(off)) for i, off in enumerate(OFFS)]

    def start_dk(step, sent):
        wait(sent)
        own = slice(256, 512)
        r.air_dx[:, own] += r.ret_a_in[step, 1] * low_on
        own = slice(SL, SL + 256)
        r.air_dx[:, own] += r.ret_a_in[step, 0] * up_on
        for hi in range(8):
            r.pay_dk[step, hi : hi + 1, :] = r.air_dx[8:9, 256 + hi * 128 : 256 + (hi + 1) * 128]
        sent = [send(r.pay_dk.at[step], r.in_dk.at[step, i], near(off)) for i, off in enumerate(OFFS)]
        r.air_cot[0:8, :] += r.air_dx[0:8, 256 : 256 + SL]
        return sent

    def finish_sea_cot(step, sent):
        wait(sent[2:4])
        r.sea_cot[...] += (
            r.sea_dx[0:48, SL : 2 * SL]
            + r.ret_s_in[step, 1].astype(F32) * low_on
            + r.ret_s_in[step, 0].astype(F32) * up_on
        )

    def finish_dg(step, sent):
        wait(sent)
        r.tmp32[...] = regrid(
            field_of(r.pay_dg, r.in_dg, step, True), True,
            r.oh_as, a_sea, r.oh_aa, a_air, lambda k: air_meta(k, 2),
        )
        for hi in range(8):
            r.air_cot[8:12, hi * 128 : (hi + 1) * 128] = r.tmp32[hi * 4 : hi * 4 + 4, :]

    def finish_dk(step, sent):
        wait(sent)
        r.tmp8[...] = regrid(
            field_of(r.pay_dk, r.in_dk, step, False), False,
            r.oh_sa, s_air, r.oh_ss, s_sea, lambda k: own_weight(k, 1),
        )
        for hi in range(8):
            r.sea_cot[0:1, hi * 128 : (hi + 1) * 128] += r.tmp8[hi : hi + 1, :]

    wait(own_sea)
    halo_sea = [
        send(r.halo_s_in.at[0, 1], r.halo_s_in.at[0, off + 1], near(off)) for off in (-1, 1)
    ]
    sent_k = regrid_surface(0, sent_s)
    sent_g = regrid_flux(0, sent_f)
    sent_cot = [give(r.cota, r.cota_in, served(0)), give(r.cots, r.cots_in, served(0))]
    air_states(0, halo_air)
    sea_states(0, halo_sea)
    air_forward(0, sent_k)
    for hi in range(8):
        r.new_f[hi * 4 : hi * 4 + 4, :] = r.air_out[8:12, hi * 128 : (hi + 1) * 128]
    r.pay_f[1] = r.new_f[...].astype(BF)
    sent_f = start_f(1)
    halo_air = start_halo_air(1)
    sea_forward(0, sent_g)
    sent_s = start_s(1)
    halo_sea = start_halo_sea(1)

    air_states(1, halo_air)
    sent_g = regrid_flux(1, sent_f)
    sea_states(1, halo_sea)
    sent_k = regrid_surface(1, sent_s)
    sea_forward(1, sent_g)
    wait(sent_cot)
    r.sea_cot[...] = r.cots_in[...].astype(F32)
    r.air_cot[0:8, :] = r.cota_in[...]
    r.air_cot[8:16, :] = jnp.zeros((8, SL), F32)
    backward(SEA, 1)
    sea_c = start_c_sea(1)
    air_forward(1, sent_k)
    backward(AIR, 1)
    air_c = start_c_air(1)

    weight_grads(SEA, 1)
    sent_dg = start_dg(1, sea_c)
    weight_grads(AIR, 1)
    finish_sea_cot(1, sea_c)
    sent_dk = start_dk(1, air_c)
    r.back_sea[...] = r.o_now[...].astype(BF)
    home = [give(r.a_now, r.home_air, band), give(r.back_sea, r.home_sea, band)]
    finish_dg(1, sent_dg)
    backward(AIR, 0)
    air_c = start_c_air(0)
    weight_grads(AIR, 0)
    finish_dk(1, sent_dk)
    backward(SEA, 0)
    sea_c = start_c_sea(0)
    weight_grads(SEA, 0)

    for c in range(2):
        for y in range(4):
            for e in range(8):
                start = ((c * 4 + y) * 8 + e) * 16
                r.gb[c, y, e] = r.g32[start : start + 16, :].astype(BF)
    sum_core = [send(r.gb.at[1 - core], r.r1, peer_core)]
    sent_dk = start_dk(0, air_c)
    wait(sum_core)
    r.h1[...] = (r.gb[core].astype(F32) + r.r1[...].astype(F32)).astype(BF)
    sum_y = [
        send(r.h1.at[lax.rem(yy + s, 4)], r.r2.at[s - 1], peers_y[s - 1]) for s in (1, 2, 3)
    ]
    wait(home)
    for row in range(8):
        r.o_air[:, row, :] = r.home_air[:, row * 128 : (row + 1) * 128]
    for row in range(2):
        r.o_sea[:, row, :] = r.home_sea[:, row * 512 : (row + 1) * 512].astype(F32)
    sent_dg = start_dg(0, sea_c)
    wait(sum_y)
    h2 = r.h1[yy].astype(F32)
    for s in range(3):
        h2 = h2 + r.r2[s].astype(F32)
    h2 = h2.astype(BF)
    r.h2[...] = h2
    r.r3[xx] = h2
    sum_x = [send(r.h2, r.r3.at[xx], dev) for dev in peers_x]
    finish_sea_cot(0, sea_c)
    finish_dk(0, sent_dk)
    r.back_dsea[...] = r.sea_cot[...].astype(BF)
    wait(sum_x)
    h3 = r.r3[0].astype(F32)
    for s in range(1, nx):
        h3 = h3 + r.r3[s].astype(F32)
    h3 = h3.astype(BF)
    r.h3[...] = h3
    r.r4[zz] = h3
    sum_z = [send(r.h3, r.r4.at[zz], dev) for dev in peers_z]
    finish_dg(0, sent_dg)
    home = [give(r.air_cot, r.home_dair, band), give(r.back_dsea, r.home_dsea, band)]
    wait(sum_z)
    h4 = r.r4[0].astype(F32)
    for s in range(1, nz):
        h4 = h4 + r.r4[s].astype(F32)
    r.gout[core, yy] = h4.astype(BF)
    give_y = [send(r.gout.at[core, yy], r.gout.at[core, yy], dev) for dev in peers_y]
    wait(home)
    for row in range(8):
        lanes = slice(row * 128, (row + 1) * 128)
        r.o_dair[:, row, :] = r.home_dair[0:8, lanes]
        r.o_dflux[:, row, :] = r.home_dair[8:12, lanes]
    for row in range(2):
        r.o_dsea[:, row, :] = r.home_dsea[:, row * 512 : (row + 1) * 512].astype(F32)
    wait(give_y)
    give_core = [send(r.gout.at[core], r.gout.at[core], peer_core)]
    wait(give_core)
    r.o_grads[...] = r.gout[...]


def finish(n, *refs):
    given, results = refs[0:5], refs[6:11]
    r = Names(
        ("grads",) + tuple("o_" + m + "_" + w for m in ("air", "sea") for w in WEIGHTS) + ("g32",),
        (refs[5],) + refs[11:],
    )
    for a, b in zip(given, results):
        b[...] = a[...]
    for c in range(2):
        for y in range(4):
            for e in range(8):
                start = ((c * 4 + y) * 8 + e) * 16
                r.g32[start : start + 16, :] = r.grads[c, y, e].astype(F32)

    scale = 1.0 / math.sqrt(SL * n)
    for m in (AIR, SEA):
        o = lambda s: getattr(r, "o_" + m.name + "_" + s)
        col = 0 if m is SEA else 64
        for half in range(2):
            start = G_EXP + 2 * col + half * 64
            o("exp")[:, half * 128 : (half + 1) * 128] = r.g32[start : start + 64, :] * scale
            start = G_CON + 2 * col + half * 64
            o("con")[:, half * 128 : (half + 1) * 128] = r.g32[start : start + 64, :] * scale
        start = G_DEC + (0 if m is SEA else 48)
        count_out = 48 if m is SEA else 12
        o("dec")[...] = r.g32[start : start + count_out, 0:64] * scale
        shift = 0 if m is SEA else 16
        o("dw")[...] = (jnp.transpose(r.g32[G_DW : G_DW + 64, :]) * scale)[shift : shift + 9, :]
        chans = 52 if m is SEA else 9
        for i in range(3):
            for j in range(3):
                t = 3 * i + j
                if m is AIR:
                    base, left = G_ENC1, 64 + 16 * j
                else:
                    base, left = (G_ENC0, 64 * j) if j < 2 else (G_ENC1, 0)
                piece = r.g32[base + i * 64 : base + (i + 1) * 64, left : left + chans]
                o("enc")[:, t * chans : (t + 1) * chans] = piece * scale


def body(n, *args):
    (
        air_state, sea_state, flux, air_cells, sea_cells, counts, sea_share, air_share, partner, wet,
        air_c, sea_c, air_enc, air_dw, air_exp, air_con, air_dec, sea_enc, sea_dw, sea_exp, sea_con,
        sea_dec,
    ) = args
    slots = lambda x: jnp.transpose(x, (1, 0, 2))
    given = [
        air_state, sea_state, flux, slots(air_cells), slots(sea_cells), counts, slots(sea_share),
        slots(air_share), partner[None], wet, air_c, sea_c,
        air_enc, air_dw.T, air_exp.T, air_con, air_dec, sea_enc, sea_dw.T, sea_exp.T, sea_con, sea_dec,
    ]
    vmem = pl.BlockSpec(memory_space=pltpu.VMEM)
    fields = [jax.ShapeDtypeStruct(x.shape, F32) for x in (air_state, sea_state, air_c, sea_c, flux)]
    made = pl.pallas_call(
        lambda *refs: kernel(n, *refs),
        out_shape=fields + [jax.ShapeDtypeStruct((2, 4, 8, 16, 128), BF)],
        in_specs=[vmem] * len(given),
        out_specs=[vmem] * 6,
        scratch_shapes=[pltpu.VMEM(shape, kind) for _, shape, kind in scratch_list()]
        + [pltpu.SemaphoreType.DMA((COPIES,)), pltpu.SemaphoreType.DMA((COPIES,))],
        compiler_params=pltpu.CompilerParams(
            collective_id=0, has_side_effects=True, vmem_limit_bytes=60 * 1024 * 1024
        ),
        name="coupled",
    )(*given)
    grads = [air_enc, air_dw.T, air_exp.T, air_con, air_dec, sea_enc, sea_dw.T, sea_exp.T, sea_con, sea_dec]
    done = pl.pallas_call(
        lambda *refs: finish(n, *refs),
        out_shape=fields + [jax.ShapeDtypeStruct(x.shape, F32) for x in grads],
        in_specs=[vmem] * 6,
        out_specs=[vmem] * 15,
        scratch_shapes=[pltpu.VMEM((GROWS, 128), F32)],
        name="finish",
    )(*made)
    done = list(done)
    for i in (6, 7, 11, 12):
        done[i] = done[i].T
    return done


def solution(mesh):
    n = mesh.shape["tile"]
    rows = P(None, "tile", None)
    slots = P("tile", None, None)
    return jax.shard_map(
        lambda *args: tuple(body(n, *args)),
        mesh=mesh,
        in_specs=(rows, rows, rows, slots, slots, P("tile", None), slots, slots, P(), P("tile", None), rows, rows)
        + (P(),) * 10,
        out_specs=(rows,) * 5 + (P(),) * 10,
        check_vma=False,
    )
```
